32 devices in a mesh: seq: 16 (over z, y, core), head: 2 (over x).
Axes of the slice: x: 2, y: 2, z: 4, core: 2. Of those that a mesh axis runs over, the one named last changes fastest.
Arguments:
- queries: bfloat16 [2048, 8192], P('seq', 'head'), may hold values from -48 to 48
- keyval: bfloat16 [2048, 2048], P('seq', 'head'), may hold values from -48 to 48
- grad_out: bfloat16 [2048, 8192], P('seq', 'head'), may hold values from -6 to 6
- doc_ids: int32 [2048], P('seq'), may hold values from 0 to 3, never falling along the last dimension, each value on 1 to 1024 neighbouring positions
- deltas: bfloat16 [2, 2048, 8192], P('head', 'seq'), may hold values from -6 to 6
- node_weights: bfloat16 [8192, 2048], P('head', 'seq'), may hold values from -0.0625 to 0.0625
- layer_slot: int32 [2], replicated, may hold values from 0 to 1, each once
Outputs:
- grad_query: bfloat16 [2048, 8192], P('seq', 'head')
- grad_keyval: bfloat16 [2048, 2048], P('seq', 'head')
- scores: float32 [2, 16], replicated
The draws below stay inside these ranges and needn't reach their ends.
Inputs may be any that keep to these rules, and one draw needn't show every extreme that they name: `layer_slot`: each of the 2 layers stands in exactly one slot. `doc_ids`: never falling along the sequence.
All inputs are finite; a program needn't handle non-finite values.
Results may differ from the reference program's by a relative error of at most 0.013.
Values may be sent and summed in bfloat16 or wider, within the bound.
No kernel may reach another device: no remote copies, remote signals or barrier semaphores. Data moves between devices by JAX's collectives and lax.ppermute only.
A program may use at most 128 MiB of HBM per device.

```python
import math
import jax
import jax.numpy as jnp
import numpy as np
from jax import lax

D = 8192
H = 64
KVH = 8
HD = 128
SEQ = 2048
LAYERS = 2


def attention_pair(key):
    base = jax.random.fold_in(key, 7)
    key_query, key_keys = jax.random.split(base, 2)
    queries = jnp.clip(jax.random.normal(key_query, (SEQ, H * HD), jnp.float32), -4.0, 4.0)
    keyval = jnp.clip(jax.random.normal(key_keys, (SEQ, KVH * 2 * HD), jnp.float32), -4.0, 4.0)
    return (queries, keyval)


def draw_queries(key, part):
    return attention_pair(key)[0].astype(jnp.bfloat16)


def draw_keyval(key, part):
    return attention_pair(key)[1].astype(jnp.bfloat16)


def levels(key, dims, cuts, smallest, largest):
    def one(dim, shards_of):
        steps = jax.random.uniform(jax.random.fold_in(jax.random.fold_in(key, 6), dim), (shards_of,), jnp.float32, smallest / len(cuts), largest / len(cuts))
        return jnp.repeat(jnp.exp(steps), dims[dim] // shards_of).reshape((-1,) + (1,) * (len(dims) - dim - 1))

    loudness = one(*cuts[0])
    for cut in cuts[1:]:
        loudness = loudness * one(*cut)
    return loudness


def profile(count, total, most, skew):
    weights = [(1 << 20) // math.isqrt(grade ** skew) + 1 for grade in range(2, count + 1)]
    rest, counts = total - most - (count - 1), [1] * (count - 1)
    while rest > 0:
        candidates = [i for i in range(count - 1) if counts[i] < most]
        whole, budget = sum([weights[i] for i in candidates]), rest
        for i in candidates:
            more = min(most - counts[i], max(1, budget * weights[i] // whole), rest)
            counts[i] = counts[i] + more
            rest = rest - more
    return np.array([most] + counts)


def ragged_sizes(own_key, number_of, total, bound, skew):
    if number_of == 2:
        one = jax.random.randint(own_key, (), max(1, total - bound), min(bound, total - 1) + 1)
        return jnp.stack([one, total - one])
    lengths = jnp.asarray(profile(number_of, total, bound, skew), jnp.int32)
    pairs = (number_of - 1) // 2
    donor, receiver = lengths[1:1 + 2 * pairs:2], lengths[2:2 + 2 * pairs:2]
    slack = jnp.minimum(donor - 1, bound - receiver)
    moved = jax.random.randint(jax.random.fold_in(own_key, 1), (pairs,), 0, 1 << 20) % (slack + 1)
    lengths = lengths.at[1:1 + 2 * pairs:2].set(donor - moved).at[2:2 + 2 * pairs:2].set(receiver + moved)
    return lengths[jax.random.permutation(jax.random.fold_in(own_key, 2), number_of)]


def scatter_about(key, dims, width, bound, cuts=(), kind=jnp.bfloat16):
    drawn = jax.random.normal(key, dims, jnp.float32) * width
    if len(cuts) > 0:
        drawn = levels(key, dims, cuts, -0.22, 0.18) * drawn
    return jnp.clip(drawn, min=-bound, max=bound).astype(kind)


def setup_inputs(seed: int = 0) -> dict:
    arg_keys = jax.random.split(jax.random.key(seed), 8)
    return {
        "queries": draw_queries(jax.random.fold_in(arg_keys[7], 71), 0),
        "keyval": draw_keyval(jax.random.fold_in(arg_keys[7], 71), 0),
        "grad_out": scatter_about(arg_keys[2], (SEQ, H * HD), 1.0, 6.0, ((0, 16), (1, 2))),
        "doc_ids": jnp.searchsorted(jnp.cumsum(ragged_sizes(arg_keys[3], 4, SEQ, SEQ // 2, 0)), jnp.arange(SEQ), side="right").astype(jnp.int32),
        "deltas": scatter_about(arg_keys[4], (LAYERS, SEQ, D), 1.0, 6.0, ((0, 2), (1, 16))),
        "node_weights": scatter_about(arg_keys[5], (D, KVH * 2 * HD), D ** -0.5, 0.0625, ((0, 2), (1, 16))),
        "layer_slot": jax.random.permutation(arg_keys[6], LAYERS).astype(jnp.int32),
    }


def reference(queries, keyval, grad_out, doc_ids, deltas, node_weights, layer_slot):
    group_size = H // KVH
    score_scale = 1.0 / math.sqrt(HD)
    positions = jnp.arange(SEQ, dtype=jnp.int32)
    allowed = (doc_ids[None, :] == doc_ids[:, None]) & (positions[None, :] <= positions[:, None])
    query_grid = queries.reshape(SEQ, KVH, group_size, HD)
    out_grid = grad_out.reshape(SEQ, KVH, group_size, HD)
    kv_grid = keyval.reshape(SEQ, KVH, 2, HD)

    def one_group(group_index):
        key_rows = kv_grid[:, group_index, 0]
        value_rows = kv_grid[:, group_index, 1]

        def one_head(head_index):
            query_rows = query_grid[:, group_index, head_index]
            out_rows = out_grid[:, group_index, head_index]
            logits = jnp.dot(query_rows, key_rows.T, preferred_element_type=jnp.float32) * score_scale
            logits = jnp.where(allowed, logits, -jnp.inf)
            row_max = lax.optimization_barrier(jnp.max(logits, axis=1, keepdims=True))
            weights = jnp.exp(logits - row_max)
            probs = weights / lax.optimization_barrier(jnp.sum(weights, axis=1, keepdims=True))
            attn_out = jnp.dot(probs, value_rows.astype(jnp.float32), precision=lax.Precision.HIGHEST)
            row_dot = lax.optimization_barrier(jnp.sum(out_rows.astype(jnp.float32) * attn_out, axis=1, keepdims=True))
            probs_low = probs.astype(jnp.bfloat16)
            grad_probs = jnp.dot(out_rows, value_rows.T, preferred_element_type=jnp.float32)
            grad_logits = (probs * (grad_probs - row_dot)).astype(jnp.bfloat16)
            grad_q = jnp.dot(grad_logits, key_rows, preferred_element_type=jnp.float32) * score_scale
            grad_k = jnp.dot(grad_logits.T, query_rows, preferred_element_type=jnp.float32) * score_scale
            grad_v = jnp.dot(probs_low.T, out_rows, preferred_element_type=jnp.float32)
            return (grad_q.astype(jnp.bfloat16), grad_k, grad_v)
        grad_q, grad_k, grad_v = lax.map(one_head, jnp.arange(group_size))
        return (grad_q, lax.optimization_barrier(jnp.sum(grad_k, axis=0)), lax.optimization_barrier(jnp.sum(grad_v, axis=0)))
    grad_q, grad_k, grad_v = lax.map(one_group, jnp.arange(KVH))
    grad_query = jnp.transpose(grad_q, (2, 0, 1, 3)).reshape(SEQ, H * HD)
    grad_both = jnp.stack((grad_k, grad_v), axis=1)
    grad_keyval = jnp.transpose(grad_both, (2, 0, 1, 3)).reshape(SEQ, KVH * 2 * HD).astype(jnp.bfloat16)
    node_count = 2 * KVH
    grad_nodes = grad_keyval.reshape(SEQ, node_count, HD)
    weight_nodes = node_weights.reshape(D, node_count, HD)

    def one_node(node_index):
        node_grad = jnp.dot(grad_nodes[:, node_index], weight_nodes[:, node_index].T, preferred_element_type=jnp.float32)

        def one_layer(slot_index):
            return jnp.sum(deltas[slot_index].astype(jnp.float32) * node_grad)
        return lax.map(one_layer, jnp.arange(LAYERS))
    slot_scores = lax.map(one_node, jnp.arange(node_count)).T / math.sqrt(SEQ)
    placing = (layer_slot[:, None] == jnp.arange(LAYERS, dtype=jnp.int32)[None, :]).astype(jnp.float32)
    scores = jnp.dot(placing.T, slot_scores, precision=lax.Precision.HIGHEST)
    return (grad_query, grad_keyval, scores)
```

```python
import functools
import math

import jax
import jax.numpy as jnp
from jax import lax
from jax.experimental import pallas as pl
from jax.experimental.pallas import tpu as pltpu
from jax.sharding import PartitionSpec as P

H = 64
KVH = 8
HD = 128
DOC_ROWS = 16
NEG = -1e30
ANY = pl.BlockSpec(memory_space=pl.ANY)
SMEM = pl.BlockSpec(memory_space=pltpu.SMEM)
VMEM = pl.BlockSpec(memory_space=pltpu.VMEM)
F32 = jnp.float32
BF16 = jnp.bfloat16


def head_of(member, members, per_head):
    fold = min(per_head, members)
    return lax.div(member, fold) + lax.rem(member, fold) * (members // fold)


def cols(index, width):
    return pl.ds(pl.multiple_of(index * width, width), width)


def run_copies(copies):
    for copy in copies:
        copy.start()
    for copy in copies:
        copy.wait()


def pack_keys_kernel(members, per_head, place_ref, doc_ref, kv_ref, *outs):
    tok = kv_ref.shape[0]
    ids = (doc_ref[...] + 1).astype(F32)
    ids = jnp.concatenate([ids] * (2 * HD // tok), axis=1)
    for r, out in enumerate(outs):
        head = head_of(place_ref[0] ^ r, members, per_head)
        out[:tok, :] = kv_ref[:, cols(head, 2 * HD)]
        out[tok:, :] = jnp.broadcast_to(ids, (DOC_ROWS, 2 * HD)).astype(BF16)


def pack_keys(place, doc_ids, keyval, members, per_head):
    tok = keyval.shape[0]
    return pl.pallas_call(
        functools.partial(pack_keys_kernel, members, per_head),
        out_shape=[jax.ShapeDtypeStruct((tok + DOC_ROWS, 2 * HD), BF16)] * members,
        in_specs=[SMEM, VMEM, VMEM],
        out_specs=[VMEM] * members,
        name="pack_keys",
    )(place, doc_ids.reshape(1, tok), keyval)


def pack_queries_kernel(members, per_head, width, place_ref, q_ref, o_ref, *outs):
    tok = q_ref.shape[0]
    for r, out in enumerate(outs):
        head = head_of(place_ref[0] ^ (r + 1), members, per_head)
        out[:tok, :] = q_ref[:, cols(head, width)]
        out[tok:, :] = o_ref[:, cols(head, width)]


def pack_queries(place, queries, grad_out, members, per_head, width):
    if members == 1:
        return []
    return pl.pallas_call(
        functools.partial(pack_queries_kernel, members, per_head, width),
        out_shape=[jax.ShapeDtypeStruct((2 * queries.shape[0], width), BF16)] * (members - 1),
        in_specs=[SMEM, VMEM, VMEM],
        out_specs=[VMEM] * (members - 1),
        name="pack_queries",
    )(place, queries, grad_out)


def split_kernel(place_ref, d_ref, mine_ref, theirs_ref):
    width = mine_ref.shape[1]
    mine_ref[...] = d_ref[:, cols(place_ref[1], width)]
    theirs_ref[...] = d_ref[:, cols(1 - place_ref[1], width)]


def split_width(place, rows):
    half = jax.ShapeDtypeStruct((rows.shape[0], rows.shape[1] // 2), BF16)
    return pl.pallas_call(
        split_kernel,
        out_shape=[half, half],
        in_specs=[SMEM, VMEM],
        out_specs=[VMEM, VMEM],
        name="split_deltas",
    )(place, rows)


def attention_kernel(members, per_head, group_size, tok, back, window, n_after, *refs):
    n_kv = back + 1
    n_in = 2 + members + n_kv
    refs = refs[:n_in] + refs[n_in + n_after :]
    place_ref, q_ref, o_ref = refs[:3]
    qo_refs = refs[3 : 2 + members]
    kv_refs = refs[2 + members : 2 + members + n_kv]
    outs = refs[2 + members + n_kv :]
    dq_outs, own_out, prev_outs = outs[:members], outs[members], outs[members + 1 : members + 1 + back]
    qs, dos, kvs, docs, k_t, bias, dqs, dk, dv, sems = outs[members + 1 + back :]
    plane = members * tok
    me = place_ref[0]
    width = group_size * HD
    tile = bias.shape[2]
    span = bias.shape[1]
    n_tiles = plane // tile
    copies = []

    def add(src, dst):
        copies.append(pltpu.make_async_copy(src, dst, sems.at[len(copies)]))

    def rows(shard, size=None):
        size = tok if size is None else size
        return pl.ds(pl.multiple_of(shard * size, size), size)

    for r in range(members):
        shard = me ^ r
        for b in range(n_kv):
            at = (back - b) * members + shard
            add(kv_refs[b].at[r, pl.ds(0, tok), :], kvs.at[rows(at), :])
            add(kv_refs[b].at[r, pl.ds(tok, DOC_ROWS), :], docs.at[rows(at, DOC_ROWS), :])
    head = head_of(me, members, per_head)
    add(q_ref.at[:, cols(head, width)], qs.at[rows(me), :])
    add(o_ref.at[:, cols(head, width)], dos.at[rows(me), :])
    for r in range(1, members):
        add(qo_refs[r - 1].at[pl.ds(0, tok), :], qs.at[rows(me ^ r), :])
        add(qo_refs[r - 1].at[pl.ds(tok, tok), :], dos.at[rows(me ^ r), :])
    for copy in copies:
        copy.start()
    dk[...] = jnp.zeros_like(dk)
    dv[...] = jnp.zeros_like(dv)
    for copy in copies[: 2 * members * n_kv]:
        copy.wait()

    n_blocks = n_kv * plane // tok
    eye = lax.broadcasted_iota(jnp.int32, (tok, tok), 0) == lax.broadcasted_iota(jnp.int32, (tok, tok), 1)
    for b in range(n_blocks):
        k_t[:, b * tok : (b + 1) * tok] = kvs[b * tok : (b + 1) * tok, :HD].astype(F32).T.astype(BF16)
    first = back * plane - window

    def doc_row(b):
        return docs[b * DOC_ROWS : (b + 1) * DOC_ROWS, :tok].astype(F32)[:1]

    for b in range(n_blocks):
        column = jnp.sum(jnp.where(eye, jnp.broadcast_to(doc_row(b), (tok, tok)), 0.0), axis=1, keepdims=True)
        for i in range(n_tiles):
            low = first + i * tile
            if b * tok < low or b * tok >= low + span:
                continue
            at = b * tok - low
            here = back * plane + i * tile
            q_row = jnp.concatenate([doc_row(here // tok + k) for k in range(tile // tok)], axis=1)
            key_pos = b * tok + lax.broadcasted_iota(jnp.int32, (tok, tile), 0)
            query_pos = here + lax.broadcasted_iota(jnp.int32, (tok, tile), 1)
            ok = (column == q_row) & (key_pos <= query_pos)
            bias[i, at : at + tok, :] = jnp.where(ok, 0.0, NEG)
    for copy in copies[2 * members * n_kv :]:
        copy.wait()

    scale = 1.0 / math.sqrt(HD)
    to_log2 = scale * math.log2(math.e)
    nt = (((1,), (1,)), ((), ()))

    def one_head(h, _):
        at_h = cols(h, HD)
        for i in range(n_tiles):
            low = first + i * tile
            q = qs[i * tile : (i + 1) * tile, at_h]
            do = dos[i * tile : (i + 1) * tile, at_h]
            keys = kvs[low : low + span, :HD]
            values = kvs[low : low + span, HD:]
            st = lax.dot_general(keys, q, nt, preferred_element_type=F32) * to_log2 + bias[i]
            top = jnp.max(st, axis=0, keepdims=True)
            e = jnp.exp2(st - top)
            inv = 1.0 / jnp.sum(e, axis=0, keepdims=True)
            dpt = lax.dot_general(values, do, nt, preferred_element_type=F32)
            p = e * inv
            row_dot = jnp.sum(p * dpt, axis=0, keepdims=True)
            ds = (p * (dpt - row_dot)).astype(BF16)
            dv[low : low + span, :] += jnp.dot(p.astype(BF16), do, preferred_element_type=F32)
            dk[low : low + span, :] += jnp.dot(ds, q, preferred_element_type=F32)
            dqt = jnp.dot(k_t[:, low : low + span], ds, preferred_element_type=F32)
            dqs[i * tile : (i + 1) * tile, at_h] = (dqt.T * scale).astype(BF16)
        return 0

    lax.fori_loop(0, group_size, one_head, 0)
    own_out[:, :HD] = dk[back * plane :, :] * scale
    own_out[:, HD:] = dv[back * plane :, :]
    for b in range(1, n_kv):
        low = (back - b) * plane
        prev_outs[b - 1][:, :HD] = (dk[low : low + plane, :] * scale).astype(BF16)
        prev_outs[b - 1][:, HD:] = dv[low : low + plane, :].astype(BF16)
    run_copies(
        [pltpu.make_async_copy(dqs.at[rows(me ^ r), :], dq_outs[r], sems.at[r]) for r in range(members)]
    )


def attention(place, queries, grad_out, qo, kv, members, per_head, group_size, window, after):
    tok = queries.shape[0]
    plane = members * tok
    back = len(kv) - 1
    tile = min(256, plane)
    span = window + tile
    keys = (back + 1) * plane
    width = group_size * HD
    n_copies = 2 * members * len(kv) + 2 * members
    flops = 40 * group_size * plane * span * HD
    return pl.pallas_call(
        functools.partial(attention_kernel, members, per_head, group_size, tok, back, window, len(after)),
        out_shape=[jax.ShapeDtypeStruct((tok, width), BF16)] * members
        + [jax.ShapeDtypeStruct((plane, 2 * HD), F32)]
        + [jax.ShapeDtypeStruct((plane, 2 * HD), BF16)] * back,
        in_specs=[SMEM] + [ANY] * (2 + len(qo) + len(kv) + len(after)),
        out_specs=[ANY] * members + [VMEM] * (1 + back),
        scratch_shapes=[
            pltpu.VMEM((plane, width), BF16),
            pltpu.VMEM((plane, width), BF16),
            pltpu.VMEM((keys, 2 * HD), BF16),
            pltpu.VMEM((keys // tok * DOC_ROWS, 2 * HD), BF16),
            pltpu.VMEM((HD, keys), BF16),
            pltpu.VMEM((plane // tile, span, tile), F32),
            pltpu.VMEM((plane, width), BF16),
            pltpu.VMEM((keys, HD), F32),
            pltpu.VMEM((keys, HD), F32),
            pltpu.SemaphoreType.DMA((n_copies,)),
        ],
        compiler_params=pltpu.CompilerParams(vmem_limit_bytes=48 * 2**20),
        cost_estimate=pl.CostEstimate(
            flops=flops, bytes_accessed=6 * plane * width, transcendentals=group_size * plane * span
        ),
        name="attention_both_ways",
    )(place, queries, grad_out, *qo, *kv, *after)


def combine_kernel(members, tok, n_prev, place_ref, own_ref, *refs):
    prev, outs = refs[:n_prev], refs[n_prev:]
    token_outs, part_outs = outs[:members], outs[members : members + 2]
    total = outs[-1]
    g = own_ref[...]
    for part in prev:
        g = g + part[...].astype(F32)
    total[...] = g.astype(BF16)
    me = place_ref[0]
    kind = lax.rem(me, 2)
    part_outs[0][...] = total[:, cols(kind, HD)]
    part_outs[1][...] = total[:, cols(1 - kind, HD)]
    for r in range(members):
        token_outs[r][...] = total[pl.ds(pl.multiple_of((me ^ r) * tok, tok), tok), :]


def combine(place, own, prev, members, tok, after):
    plane = own.shape[0]
    n_after = len(after)

    def kernel(place_ref, own_ref, *refs):
        combine_kernel(members, tok, len(prev), place_ref, own_ref, *refs[: len(prev)], *refs[len(prev) + n_after :])

    return pl.pallas_call(
        kernel,
        out_shape=[jax.ShapeDtypeStruct((tok, 2 * HD), BF16)] * members
        + [jax.ShapeDtypeStruct((plane, HD), BF16)] * 2,
        in_specs=[SMEM] + [VMEM] * (1 + len(prev)) + [ANY] * n_after,
        out_specs=[VMEM] * (members + 2),
        scratch_shapes=[pltpu.VMEM((plane, 2 * HD), BF16)],
        name="sum_key_value_gradients",
    )(place, own, *prev, *after)


def settle_kernel(members, per_head, place_ref, *refs):
    dq, dkv = refs[:members], refs[members : 2 * members]
    out_q, out_kv = refs[2 * members :]
    for r in range(members):
        head = head_of(place_ref[0] ^ r, members, per_head)
        out_q[:, cols(head, dq[r].shape[1])] = dq[r][...]
        out_kv[:, cols(head, dkv[r].shape[1])] = dkv[r][...]


def settle(place, dq, dkv, per_head):
    members = len(dq)
    tok = dq[0].shape[0]
    return pl.pallas_call(
        functools.partial(settle_kernel, members, per_head),
        out_shape=[
            jax.ShapeDtypeStruct((tok, members * dq[0].shape[1]), BF16),
            jax.ShapeDtypeStruct((tok, members * dkv[0].shape[1]), BF16),
        ],
        in_specs=[SMEM] + [VMEM] * (2 * members),
        out_specs=[VMEM, VMEM],
        name="place_heads",
    )(place, *dq, *dkv)


def project_kernel(place_ref, *refs):
    d_refs, (w0, wa, wb0, wb1, wc0, wc1, out_ref, ds, ws, sems) = refs[:8], refs[8:]
    me, plane_at = place_ref[0], place_ref[2]
    tok = d_refs[0].shape[0]
    inner = jnp.logical_or(plane_at == 1, plane_at == 2)
    w_copies = []
    for k, pair in enumerate(((w0, w0), (wa, wa), (wb0, wb1), (wc0, wc1))):
        dst = ws.at[:, k * HD : (k + 1) * HD]
        if pair[0] is pair[1]:
            copy = pltpu.make_async_copy(pair[0], dst, sems.at[k])
            copy.start()
        else:
            copy = pltpu.make_async_copy(pair[1], dst, sems.at[k])

            @pl.when(inner)
            def _():
                pltpu.make_async_copy(pair[0], dst, sems.at[k]).start()

            @pl.when(jnp.logical_not(inner))
            def _():
                copy.start()

        w_copies.append(copy)
    copies = []
    for layer in range(2):
        for r in range(4):
            shard = layer * 4 + (me ^ r)
            dst = ds.at[pl.ds(pl.multiple_of(shard * tok, tok), tok), :]
            copies.append(pltpu.make_async_copy(d_refs[layer * 4 + r], dst, sems.at[4 + len(copies)]))
            copies[-1].start()
    for copy in w_copies + copies:
        copy.wait()
    step = 256

    def one(i, _):
        at = pl.ds(pl.multiple_of(i * step, step), step)
        out_ref[at, :] = jnp.dot(ds[at, :], ws[...], preferred_element_type=F32)
        return 0

    lax.fori_loop(0, ds.shape[0] // step, one, 0)


def project(place, pieces, blocks):
    tok, depth = pieces[0].shape
    rows = tok * len(pieces)
    return pl.pallas_call(
        project_kernel,
        out_shape=jax.ShapeDtypeStruct((rows, 4 * HD), F32),
        in_specs=[SMEM] + [ANY] * (len(pieces) + len(blocks)),
        out_specs=VMEM,
        scratch_shapes=[
            pltpu.VMEM((rows, depth), BF16),
            pltpu.VMEM((depth, 4 * HD), BF16),
            pltpu.SemaphoreType.DMA((4 + len(pieces),)),
        ],
        compiler_params=pltpu.CompilerParams(vmem_limit_bytes=48 * 2**20),
        cost_estimate=pl.CostEstimate(
            flops=2 * rows * depth * 4 * HD, bytes_accessed=2 * depth * (rows + 4 * HD), transcendentals=0
        ),
        name="project_deltas",
    )(place, *pieces, *blocks)


def contract_kernel(norm, place_ref, slot_ref, p_ref, g0, g1, g2, g3, out_ref):
    me, side, plane_at = place_ref[0], place_ref[1], place_ref[2]
    kind = lax.rem(me, 2)
    row = lax.broadcasted_iota(jnp.int32, out_ref.shape, 0)
    lane = lax.broadcasted_iota(jnp.int32, out_ref.shape, 1)
    total = jnp.zeros(out_ref.shape, F32)
    n_tok = g0.shape[0]
    for k, g_ref in enumerate((g0, g1, g2, g3)):
        block = 2 * (side ^ (k // 2)) + (kind ^ (k % 2))
        far = jnp.where(plane_at < 2, 2, 1)
        slot = jnp.where(
            block == plane_at, 0, jnp.where(block == (plane_at ^ 1), 1, jnp.where(block == far, 2, 3))
        )
        g = g_ref[...].astype(F32)
        for layer in range(2):
            part = p_ref[layer * n_tok : (layer + 1) * n_tok, cols(slot, HD)] * g
            value = jnp.sum(jnp.sum(part, axis=0, keepdims=True), axis=1, keepdims=True) * norm
            here = (row == slot_ref[side ^ layer]) & (lane == 4 * block + me)
            total = total + jnp.where(here, value, 0.0)
    out_ref[...] = total


def contract(place, layer_slot, projected, parts, norm):
    return pl.pallas_call(
        functools.partial(contract_kernel, norm),
        out_shape=jax.ShapeDtypeStruct((8, HD), F32),
        in_specs=[SMEM, SMEM] + [VMEM] * 5,
        out_specs=VMEM,
        compiler_params=pltpu.CompilerParams(vmem_limit_bytes=32 * 2**20),
        name="contract_scores",
    )(place, layer_slot, projected, *parts)


def on_device(queries, keyval, grad_out, doc_ids, deltas, node_weights, layer_slot):
    tok = queries.shape[0]
    members = keyval.shape[1] // (2 * HD)
    group_size = H // KVH
    n_seq, n_head = lax.axis_size("seq"), lax.axis_size("head")
    planes = n_seq // members
    plane_tok = members * tok
    window = n_seq * tok // 2
    back = -(-window // plane_tok)
    block_width = node_weights.shape[1]
    per_head = 2 * HD // block_width
    at_seq, at_head = lax.axis_index("seq"), lax.axis_index("head")
    place = jnp.stack([lax.rem(at_seq, members), at_head, lax.div(at_seq, members)]).astype(jnp.int32)

    def to_member(x, r):
        return lax.ppermute(x, "seq", [(s, s - s % members + ((s % members) ^ r)) for s in range(n_seq)])

    def to_plane(x, pairs):
        return lax.ppermute(
            x, "seq", [(a * members + k, b * members + k) for a, b in pairs for k in range(members)]
        )

    def shift(x, step):
        return to_plane(x, [(a, a + step) for a in range(planes) if 0 <= a + step < planes])

    def other_head(x):
        return lax.ppermute(x, "head", [(0, 1), (1, 0)])

    def other_head_and_member(x):
        pairs = [(2 * s + h, 2 * (s ^ 1) + (h ^ 1)) for s in range(n_seq) for h in range(2)]
        return lax.ppermute(x, ("seq", "head"), pairs)

    spread = n_head == 2 and members == 4 and planes == 4 and per_head == 2 and deltas.shape[0] == 1
    if spread:
        w_pair = to_plane(node_weights, [(0, 1), (1, 0), (2, 3), (3, 2)])
        w_mid = to_plane(node_weights, [(1, 2), (2, 1)])

    packed = pack_keys(place, doc_ids, keyval, members, per_head)
    kv_pieces = [packed[0]] + [to_member(packed[r], r) for r in range(1, members)]
    packed = pack_queries(place, queries, grad_out, members, per_head, group_size * HD)
    qo = [to_member(packed[r - 1], r) for r in range(1, members)]
    kv_plane = jnp.stack(kv_pieces)
    kv = [kv_plane] + [shift(kv_plane, k) for k in range(1, back + 1)]

    first, second = [], []
    if spread:
        mine, theirs = split_width(place, deltas.reshape(tok, deltas.shape[2]))
        crossed = other_head(theirs)
        near = [mine, to_member(mine, 2), crossed, to_member(crossed, 2)]
        far = [to_member(d, 1) for d in near]
        pieces = [near[0], far[0], near[1], far[1], near[2], far[2], near[3], far[3]]
        w_end = to_plane(w_mid, [(1, 0), (2, 3)])
        w_mid2 = to_plane(w_pair, [(1, 2), (2, 1)])
        w_end2 = to_plane(w_mid2, [(1, 0), (2, 3)])
        first = [w_pair, w_mid]
        second = [w_end, w_mid2]

    out = attention(place, queries, grad_out, qo, kv, members, per_head, group_size, window, first)
    dq, own, prev = out[:members], out[members], out[members + 1 :]
    prev = [shift(prev[k], -(k + 1)) for k in range(back)]
    dq = [dq[0]] + [to_member(dq[r], r) for r in range(1, members)]
    summed = combine(place, own, prev, members, tok, second)
    token_parts, kinds = summed[:members], summed[members:]
    if spread:
        parts = [kinds[0], to_member(kinds[1], 1), other_head(kinds[0]), other_head_and_member(kinds[1])]
    dkv = [token_parts[0]] + [to_member(token_parts[r], r) for r in range(1, members)]
    grad_query, grad_keyval = settle(place, dq, dkv, per_head)
    norm = 1.0 / math.sqrt(n_seq * tok)
    if spread:
        projected = project(place, pieces, [node_weights, w_pair, w_mid, w_end, w_mid2, w_end2])
        mine = contract(place, layer_slot, projected, parts, norm)
        n_dev = n_seq * n_head
        copies = lax.all_to_all(
            jnp.broadcast_to(mine[None], (n_dev,) + mine.shape), ("seq", "head"), 0, 0, tiled=True
        )
        scores = jnp.sum(copies, axis=0)[: layer_slot.shape[0], : n_seq * block_width // HD]
        return grad_query, grad_keyval, scores

    width_deltas = lax.all_to_all(deltas, "head", split_axis=2, concat_axis=0, tiled=True)
    grad_rows = lax.all_gather(grad_keyval, "head", axis=1, tiled=True)
    layer_count = width_deltas.shape[0]
    weights = lax.all_gather(node_weights, "seq", axis=1, tiled=True)
    projected = jnp.einsum("ltd,dc->ltc", width_deltas, weights, preferred_element_type=F32)
    per_column = jnp.sum(projected * grad_rows.astype(F32)[None], axis=1)
    partial_value = jnp.sum(per_column.reshape(layer_count, grad_rows.shape[1] // HD, HD), axis=2)
    totals = lax.psum(partial_value * norm, ("seq", "head"))
    placing = (layer_slot[:, None] == jnp.arange(layer_count, dtype=jnp.int32)[None, :]).astype(F32)
    scores = jnp.dot(placing.T, totals, precision=lax.Precision.HIGHEST)
    return grad_query, grad_keyval, scores


def solution(mesh):
    return jax.shard_map(
        on_device,
        mesh=mesh,
        in_specs=(
            P("seq", "head"),
            P("seq", "head"),
            P("seq", "head"),
            P("seq"),
            P("head", "seq", None),
            P("head", "seq"),
            P(),
        ),
        out_specs=(P("seq", "head"), P("seq", "head"), P()),
        check_vma=False,
    )
```

```python
import functools
import math

import jax
import jax.numpy as jnp
from jax import lax
from jax.experimental import pallas as pl
from jax.experimental.pallas import tpu as pltpu
from jax.sharding import PartitionSpec as P

H = 64
KVH = 8
HD = 128
DOC_ROWS = 16
NEG = -1e30
ANY = pl.BlockSpec(memory_space=pl.ANY)
SMEM = pl.BlockSpec(memory_space=pltpu.SMEM)
VMEM = pl.BlockSpec(memory_space=pltpu.VMEM)
F32 = jnp.float32
BF16 = jnp.bfloat16


def head_of(member, members, per_head):
    fold = min(per_head, members)
    return lax.div(member, fold) + lax.rem(member, fold) * (members // fold)


def cols(index, width):
    return pl.ds(pl.multiple_of(index * width, width), width)


def run_copies(copies):
    for copy in copies:
        copy.start()
    for copy in copies:
        copy.wait()


def by_halves(outs, members):
    half = max(members // 2, 1)
    return [outs[r // half].at[r % half] for r in range(members)]


def half_shapes(members, shape, dtype):
    half = max(members // 2, 1)
    return [jax.ShapeDtypeStruct((half,) + shape, dtype)] * (members // half)


def pack_keys_kernel(members, per_head, place_ref, doc_ref, kv_ref, *outs):
    tok = kv_ref.shape[0]
    ids = (doc_ref[...] + 1).astype(F32)
    ids = jnp.concatenate([ids] * (2 * HD // tok), axis=1)
    for r, out in enumerate(by_halves(outs, members)):
        head = head_of(place_ref[0] ^ r, members, per_head)
        out[:tok, :] = kv_ref[:, cols(head, 2 * HD)]
        out[tok:, :] = jnp.broadcast_to(ids, (DOC_ROWS, 2 * HD)).astype(BF16)


def pack_keys(place, doc_ids, keyval, members, per_head):
    tok = keyval.shape[0]
    shapes = half_shapes(members, (tok + DOC_ROWS, 2 * HD), BF16)
    return pl.pallas_call(
        functools.partial(pack_keys_kernel, members, per_head),
        out_shape=shapes,
        in_specs=[SMEM, VMEM, VMEM],
        out_specs=[VMEM] * len(shapes),
        name="pack_keys",
    )(place, doc_ids.reshape(1, tok), keyval)


def pack_queries_kernel(members, per_head, width, n_after, place_ref, q_ref, o_ref, *refs):
    outs = refs[n_after:]
    tok = q_ref.shape[0]
    for r, out in enumerate(by_halves(outs, members)):
        if r == 0 and members > 2:
            continue
        head = head_of(place_ref[0] ^ r, members, per_head)
        out[:tok, :] = q_ref[:, cols(head, width)]
        out[tok:, :] = o_ref[:, cols(head, width)]


def pack_queries(place, queries, grad_out, members, per_head, width, after):
    shapes = half_shapes(members, (2 * queries.shape[0], width), BF16)
    return pl.pallas_call(
        functools.partial(pack_queries_kernel, members, per_head, width, len(after)),
        out_shape=shapes,
        in_specs=[SMEM, VMEM, VMEM] + [ANY] * len(after),
        out_specs=[VMEM] * len(shapes),
        name="pack_queries",
    )(place, queries, grad_out, *after)


def split_kernel(place_ref, d_ref, mine_ref, theirs_ref):
    width = mine_ref.shape[1]
    mine_ref[...] = d_ref[:, cols(place_ref[1], width)]
    theirs_ref[...] = d_ref[:, cols(1 - place_ref[1], width)]


def split_width(place, rows):
    half = jax.ShapeDtypeStruct((rows.shape[0], rows.shape[1] // 2), BF16)
    return pl.pallas_call(
        split_kernel,
        out_shape=[half, half],
        in_specs=[SMEM, VMEM],
        out_specs=[VMEM, VMEM],
        name="split_deltas",
    )(place, rows)


def attention_kernel(members, per_head, group_size, tok, back, window, qo_slots, n_after, *refs):
    n_kv = back + 1
    n_in = 2 + members + n_kv
    refs = refs[:n_in] + refs[n_in + n_after :]
    place_ref, q_ref, o_ref = refs[:3]
    qo_refs = [ref.at[k] for ref, k in zip(refs[3 : 2 + members], qo_slots, strict=True)]
    kv_refs = refs[2 + members : 2 + members + n_kv]
    outs = refs[2 + members + n_kv :]
    n_dq = min(members, 2)
    dq_outs = by_halves(outs[:n_dq], members)
    own_out, prev_outs = outs[n_dq], outs[n_dq + 1 : n_dq + 1 + back]
    qs, dos, kvs, docs, k_t, bias, dqs, dk, dv, sems = outs[n_dq + 1 + back :]
    plane = members * tok
    me = place_ref[0]
    width = group_size * HD
    tile = bias.shape[2]
    span = bias.shape[1]
    n_tiles = plane // tile
    copies = []

    def add(src, dst):
        copies.append(pltpu.make_async_copy(src, dst, sems.at[len(copies)]))

    def rows(shard, size=None):
        size = tok if size is None else size
        return pl.ds(pl.multiple_of(shard * size, size), size)

    for r in range(members):
        shard = me ^ r
        for b in range(n_kv):
            at = (back - b) * members + shard
            add(kv_refs[b].at[r, pl.ds(0, tok), :], kvs.at[rows(at), :])
            add(kv_refs[b].at[r, pl.ds(tok, DOC_ROWS), :], docs.at[rows(at, DOC_ROWS), :])
    head = head_of(me, members, per_head)
    add(q_ref.at[:, cols(head, width)], qs.at[rows(me), :])
    add(o_ref.at[:, cols(head, width)], dos.at[rows(me), :])
    for r in range(1, members):
        add(qo_refs[r - 1].at[pl.ds(0, tok), :], qs.at[rows(me ^ r), :])
        add(qo_refs[r - 1].at[pl.ds(tok, tok), :], dos.at[rows(me ^ r), :])
    for copy in copies:
        copy.start()
    dk[...] = jnp.zeros_like(dk)
    dv[...] = jnp.zeros_like(dv)
    for copy in copies[: 2 * members * n_kv]:
        copy.wait()

    n_blocks = n_kv * plane // tok
    eye = lax.broadcasted_iota(jnp.int32, (tok, tok), 0) == lax.broadcasted_iota(jnp.int32, (tok, tok), 1)
    for b in range(n_blocks):
        k_t[:, b * tok : (b + 1) * tok] = kvs[b * tok : (b + 1) * tok, :HD].astype(F32).T.astype(BF16)
    first = back * plane - window

    def doc_row(b):
        return docs[b * DOC_ROWS : (b + 1) * DOC_ROWS, :tok].astype(F32)[:1]

    for b in range(n_blocks):
        column = jnp.sum(jnp.where(eye, jnp.broadcast_to(doc_row(b), (tok, tok)), 0.0), axis=1, keepdims=True)
        for i in range(n_tiles):
            low = first + i * tile
            if b * tok < low or b * tok >= low + span:
                continue
            at = b * tok - low
            here = back * plane + i * tile
            q_row = jnp.concatenate([doc_row(here // tok + k) for k in range(tile // tok)], axis=1)
            key_pos = b * tok + lax.broadcasted_iota(jnp.int32, (tok, tile), 0)
            query_pos = here + lax.broadcasted_iota(jnp.int32, (tok, tile), 1)
            ok = (column == q_row) & (key_pos <= query_pos)
            bias[i, at : at + tok, :] = jnp.where(ok, 0.0, NEG)
    for copy in copies[2 * members * n_kv :]:
        copy.wait()

    scale = 1.0 / math.sqrt(HD)
    to_log2 = scale * math.log2(math.e)
    nt = (((1,), (1,)), ((), ()))

    def one_head(h, _):
        at_h = cols(h, HD)
        for i in range(n_tiles):
            low = first + i * tile
            q = qs[i * tile : (i + 1) * tile, at_h]
            do = dos[i * tile : (i + 1) * tile, at_h]
            keys = kvs[low : low + span, :HD]
            values = kvs[low : low + span, HD:]
            st = lax.dot_general(keys, q, nt, preferred_element_type=F32) * to_log2 + bias[i]
            top = jnp.max(st, axis=0, keepdims=True)
            e = jnp.exp2(st - top)
            inv = 1.0 / jnp.sum(e, axis=0, keepdims=True)
            dpt = lax.dot_general(values, do, nt, preferred_element_type=F32)
            p = e * inv
            row_dot = jnp.sum(p * dpt, axis=0, keepdims=True)
            ds = (p * (dpt - row_dot)).astype(BF16)
            dv[low : low + span, :] += jnp.dot(p.astype(BF16), do, preferred_element_type=F32)
            dk[low : low + span, :] += jnp.dot(ds, q, preferred_element_type=F32)
            dqt = jnp.dot(k_t[:, low : low + span], ds, preferred_element_type=F32)
            dqs[i * tile : (i + 1) * tile, at_h] = (dqt.T * scale).astype(BF16)
        return 0

    lax.fori_loop(0, group_size, one_head, 0)
    own_out[:, :HD] = dk[back * plane :, :] * scale
    own_out[:, HD:] = dv[back * plane :, :]
    for b in range(1, n_kv):
        low = (back - b) * plane
        prev_outs[b - 1][:, :HD] = (dk[low : low + plane, :] * scale).astype(BF16)
        prev_outs[b - 1][:, HD:] = dv[low : low + plane, :].astype(BF16)
    run_copies(
        [pltpu.make_async_copy(dqs.at[rows(me ^ r), :], dq_outs[r], sems.at[r]) for r in range(members)]
    )


def attention(place, queries, grad_out, qo, kv, members, per_head, group_size, window, after):
    tok = queries.shape[0]
    plane = members * tok
    back = len(kv) - 1
    tile = min(256, plane)
    span = window + tile
    keys = (back + 1) * plane
    width = group_size * HD
    n_copies = 2 * members * len(kv) + 2 * members
    flops = 2 * group_size * plane * span * HD
    dq_shapes = half_shapes(members, (tok, width), BF16)
    return pl.pallas_call(
        functools.partial(
            attention_kernel, members, per_head, group_size, tok, back, window, [k for _, k in qo], len(after)
        ),
        out_shape=dq_shapes
        + [jax.ShapeDtypeStruct((plane, 2 * HD), F32)]
        + [jax.ShapeDtypeStruct((plane, 2 * HD), BF16)] * back,
        in_specs=[SMEM] + [ANY] * (2 + len(qo) + len(kv) + len(after)),
        out_specs=[ANY] * len(dq_shapes) + [VMEM] * (1 + back),
        scratch_shapes=[
            pltpu.VMEM((plane, width), BF16),
            pltpu.VMEM((plane, width), BF16),
            pltpu.VMEM((keys, 2 * HD), BF16),
            pltpu.VMEM((keys // tok * DOC_ROWS, 2 * HD), BF16),
            pltpu.VMEM((HD, keys), BF16),
            pltpu.VMEM((plane // tile, span, tile), F32),
            pltpu.VMEM((plane, width), BF16),
            pltpu.VMEM((keys, HD), F32),
            pltpu.VMEM((keys, HD), F32),
            pltpu.SemaphoreType.DMA((n_copies,)),
        ],
        compiler_params=pltpu.CompilerParams(vmem_limit_bytes=24 * 2**20),
        cost_estimate=pl.CostEstimate(
            flops=flops, bytes_accessed=6 * plane * width, transcendentals=group_size * plane * span
        ),
        name="attention_both_ways",
    )(place, queries, grad_out, *[array for array, _ in qo], *kv, *after)


def combine_kernel(members, tok, n_prev, place_ref, own_ref, *refs):
    prev, outs = refs[:n_prev], refs[n_prev:]
    token_outs, part_outs = by_halves(outs[:-3], members), outs[-3:-1]
    total = outs[-1]
    g = own_ref[...]
    for part in prev:
        g = g + part[...].astype(F32)
    total[...] = g.astype(BF16)
    me = place_ref[0]
    kind = lax.rem(me, 2)
    part_outs[0][...] = total[:, cols(kind, HD)]
    part_outs[1][...] = total[:, cols(1 - kind, HD)]
    for r in range(members):
        token_outs[r][...] = total[pl.ds(pl.multiple_of((me ^ r) * tok, tok), tok), :]


def combine(place, own, prev, members, tok, after):
    plane = own.shape[0]
    n_after = len(after)
    shapes = half_shapes(members, (tok, 2 * HD), BF16)

    def kernel(place_ref, own_ref, *refs):
        combine_kernel(members, tok, len(prev), place_ref, own_ref, *refs[: len(prev)], *refs[len(prev) + n_after :])

    return pl.pallas_call(
        kernel,
        out_shape=shapes + [jax.ShapeDtypeStruct((plane, HD), BF16)] * 2,
        in_specs=[SMEM] + [VMEM] * (1 + len(prev)) + [ANY] * n_after,
        out_specs=[VMEM] * (len(shapes) + 2),
        scratch_shapes=[pltpu.VMEM((plane, 2 * HD), BF16)],
        name="sum_key_value_gradients",
    )(place, own, *prev, *after)


def settle_kernel(members, per_head, slots, place_ref, *refs):
    pieces = [ref.at[k] for ref, k in zip(refs[: 2 * members], slots, strict=True)]
    out_q, out_kv = refs[2 * members :]
    for r in range(members):
        head = head_of(place_ref[0] ^ r, members, per_head)
        for piece, out in ((pieces[r], out_q), (pieces[members + r], out_kv)):
            out[:, cols(head, piece.shape[1])] = piece[...]


def settle(place, dq, dkv, per_head):
    members = len(dq)
    tok = dq[0][0].shape[1]
    pieces = dq + dkv
    return pl.pallas_call(
        functools.partial(settle_kernel, members, per_head, [k for _, k in pieces]),
        out_shape=[
            jax.ShapeDtypeStruct((tok, members * part[0][0].shape[2]), BF16) for part in (dq, dkv)
        ],
        in_specs=[SMEM] + [VMEM] * (2 * members),
        out_specs=[VMEM, VMEM],
        name="place_heads",
    )(place, *[array for array, _ in pieces])


def project_kernel(slots, counts, place_ref, *refs):
    n_pieces, n_blocks = len(slots), sum(counts)
    d_refs = [ref.at[k] for ref, k in zip(refs[:n_pieces], slots, strict=True)]
    w_refs = refs[n_pieces : n_pieces + n_blocks]
    out_ref, ds, ws, sems = refs[n_pieces + n_blocks :]
    me, plane_at = place_ref[0], place_ref[2]
    tok = d_refs[0].shape[0]
    inner = jnp.logical_or(plane_at == 1, plane_at == 2)
    copies = []
    at = 0
    for k, count in enumerate(counts):
        dst = ws.at[:, k * HD : (k + 1) * HD]
        copies.append(pltpu.make_async_copy(w_refs[at], dst, sems.at[k]))
        if count == 1:
            copies[k].start()
        else:
            from_end = pltpu.make_async_copy(w_refs[at + 1], dst, sems.at[k])
            pl.when(inner)(copies[k].start)
            pl.when(jnp.logical_not(inner))(from_end.start)
        at += count
    for i, d_ref in enumerate(d_refs):
        shard = i // 4 * 4 + (me ^ (i % 4))
        dst = ds.at[pl.ds(pl.multiple_of(shard * tok, tok), tok), :]
        copies.append(pltpu.make_async_copy(d_ref, dst, sems.at[len(copies)]))
        copies[-1].start()
    for copy in copies:
        copy.wait()
    step = 256

    def one(i, _):
        at = pl.ds(pl.multiple_of(i * step, step), step)
        out_ref[at, :] = jnp.dot(ds[at, :], ws[...], preferred_element_type=F32)
        return 0

    lax.fori_loop(0, ds.shape[0] // step, one, 0)


def project(place, pieces, blocks):
    _, tok, depth = pieces[0][0].shape
    rows, width = tok * len(pieces), HD * len(blocks)
    arrays = [array for block in blocks for array in block]
    return pl.pallas_call(
        functools.partial(project_kernel, [k for _, k in pieces], [len(block) for block in blocks]),
        out_shape=jax.ShapeDtypeStruct((rows, width), F32),
        in_specs=[SMEM] + [ANY] * (len(pieces) + len(arrays)),
        out_specs=VMEM,
        scratch_shapes=[
            pltpu.VMEM((rows, depth), BF16),
            pltpu.VMEM((depth, width), BF16),
            pltpu.SemaphoreType.DMA((len(blocks) + len(pieces),)),
        ],
        compiler_params=pltpu.CompilerParams(vmem_limit_bytes=20 * 2**20),
        cost_estimate=pl.CostEstimate(
            flops=2 * rows * depth * width, bytes_accessed=2 * depth * (rows + width), transcendentals=0
        ),
        name="project_deltas",
    )(place, *[array for array, _ in pieces], *arrays)


def contract_kernel(norm, place_ref, slot_ref, p_ref, p_last_ref, g0, g1, g2, g3, out_ref):
    me, side, plane_at = place_ref[0], place_ref[1], place_ref[2]
    kind = lax.rem(me, 2)
    row = lax.broadcasted_iota(jnp.int32, out_ref.shape, 0)
    lane = lax.broadcasted_iota(jnp.int32, out_ref.shape, 1)
    total = jnp.zeros(out_ref.shape, F32)
    n_tok = g0.shape[0]
    for k, g_ref in enumerate((g0, g1, g2, g3)):
        block = 2 * (side ^ (k // 2)) + (kind ^ (k % 2))
        far = jnp.where(plane_at < 2, 2, 1)
        slot = jnp.where(
            block == plane_at, 0, jnp.where(block == (plane_at ^ 1), 1, jnp.where(block == far, 2, 3))
        )
        g = g_ref[...].astype(F32)
        for layer in range(2):
            rows = slice(layer * n_tok, (layer + 1) * n_tok)
            part = jnp.where(slot == 3, p_last_ref[rows, :], p_ref[rows, cols(jnp.minimum(slot, 2), HD)]) * g
            value = jnp.sum(jnp.sum(part, axis=0, keepdims=True), axis=1, keepdims=True) * norm
            here = (row == slot_ref[side ^ layer]) & (lane == 4 * block + me)
            total = total + jnp.where(here, value, 0.0)
    out_ref[...] = total


def contract(place, layer_slot, projected, parts, norm):
    return pl.pallas_call(
        functools.partial(contract_kernel, norm),
        out_shape=jax.ShapeDtypeStruct((8, HD), F32),
        in_specs=[SMEM, SMEM] + [VMEM] * 6,
        out_specs=VMEM,
        compiler_params=pltpu.CompilerParams(vmem_limit_bytes=16 * 2**20),
        name="contract_scores",
    )(place, layer_slot, *projected, *parts)


def on_device(queries, keyval, grad_out, doc_ids, deltas, node_weights, layer_slot):
    tok = queries.shape[0]
    members = keyval.shape[1] // (2 * HD)
    group_size = H // KVH
    n_seq, n_head = lax.axis_size("seq"), lax.axis_size("head")
    planes = n_seq // members
    plane_tok = members * tok
    window = n_seq * tok // 2
    back = -(-window // plane_tok)
    block_width = node_weights.shape[1]
    per_head = 2 * HD // block_width
    at_seq, at_head = lax.axis_index("seq"), lax.axis_index("head")
    place = jnp.stack([lax.rem(at_seq, members), at_head, lax.div(at_seq, members)]).astype(jnp.int32)

    def to_member(x, r):
        return lax.ppermute(x, "seq", [(s, s - s % members + ((s % members) ^ r)) for s in range(n_seq)])

    def to_plane(x, pairs):
        return lax.ppermute(
            x, "seq", [(a * members + k, b * members + k) for a, b in pairs for k in range(members)]
        )

    def shift(x, step):
        return to_plane(x, [(a, a + step) for a in range(planes) if 0 <= a + step < planes])

    def other_head(x):
        return lax.ppermute(x, "head", [(0, 1), (1, 0)])

    def other_head_and_member(x):
        pairs = [(2 * s + h, 2 * (s ^ 1) + (h ^ 1)) for s in range(n_seq) for h in range(2)]
        return lax.ppermute(x, ("seq", "head"), pairs)

    def follow(x, after):
        return lax.optimization_barrier((x, *after))[0] if after else x

    def exchange(halves, before=(), between=()):
        if members == 1:
            return [(halves[0], 0)]
        bit = members // 2
        got = to_member(follow(halves[1], before), bit)
        views = [(halves[0], r) for r in range(bit)] + [(got, r) for r in range(bit)]
        while bit > 1:
            bit //= 2
            chosen = [r for r in range(members) if r & bit]
            message = jnp.stack([views[r][0][views[r][1]] for r in chosen])
            got = to_member(follow(message, between), bit)
            for k, r in enumerate(chosen):
                views[r] = (got, k)
        return views

    spread = n_head == 2 and members == 4 and planes == 4 and per_head == 2 and deltas.shape[0] == 1
    first, second = [], []
    if spread:
        pairs, middle, ends = [(0, 1), (1, 0), (2, 3), (3, 2)], [(1, 2), (2, 1)], [(1, 0), (2, 3)]
        w_pair, w_middle = to_plane(node_weights, pairs), to_plane(node_weights, middle)
        first = [w_pair, w_middle]
        mine, theirs = split_width(place, deltas.reshape(tok, deltas.shape[2]))
        crossed = other_head(theirs)

    keys = exchange(pack_keys(place, doc_ids, keyval, members, per_head))
    kv_plane = jnp.stack([array[k] for array, k in keys])
    ready = follow(kv_plane, first)
    kv = [kv_plane] + [shift(ready, k) for k in range(1, back + 1)]
    queries_out = pack_queries(place, queries, grad_out, members, per_head, group_size * HD, ())
    qo = exchange(queries_out, [array for array, _ in keys[1:]], kv[1:])

    if spread:
        near = jnp.stack([mine, crossed])
        other = to_member(follow(near, [qo[-2][0]] + kv[1:]), 2)
        near_c = to_member(near, 1)
        w_ends = to_plane(follow(w_middle, kv[1:]), ends)
        w_middle2 = to_plane(follow(w_pair, kv[1:]), middle)
        w_ends2 = to_plane(w_middle2, ends)
        second = [w_ends, w_middle2]

    out = attention(place, queries, grad_out, qo[1:], kv, members, per_head, group_size, window, ())
    n_dq = min(members, 2)
    dq, own, prev = out[:n_dq], out[n_dq], out[n_dq + 1 :]
    prev = [shift(follow(prev[k], second), -(k + 1)) for k in range(back)]
    dq = exchange(dq)
    if spread:
        other_c = to_member(follow(other, prev), 1)
        pieces = [(array, layer) for layer in range(2) for array in (near, near_c, other, other_c)]
    summed = combine(place, own, prev, members, tok, ())
    token_parts, kinds = summed[:-2], summed[-2:]
    if spread:
        parts = [kinds[0], to_member(kinds[1], 1), other_head(kinds[0]), other_head_and_member(kinds[1])]
    dkv = exchange(token_parts)
    grad_query, grad_keyval = settle(place, dq, dkv, per_head)
    norm = 1.0 / math.sqrt(n_seq * tok)
    if spread:
        projected = [
            project(place, pieces, [(node_weights,), (w_pair,), (w_middle, w_ends)]),
            project(place, pieces, [(w_middle2, w_ends2)]),
        ]
        mine = contract(place, layer_slot, projected, parts, norm)
        n_dev = n_seq * n_head
        copies = lax.all_to_all(
            jnp.broadcast_to(mine[None], (n_dev,) + mine.shape), ("seq", "head"), 0, 0, tiled=True
        )
        scores = jnp.sum(copies, axis=0)[: layer_slot.shape[0], : n_seq * block_width // HD]
        return grad_query, grad_keyval, scores

    width_deltas = lax.all_to_all(deltas, "head", split_axis=2, concat_axis=0, tiled=True)
    grad_rows = lax.all_gather(grad_keyval, "head", axis=1, tiled=True)
    layer_count = width_deltas.shape[0]
    weights = lax.all_gather(node_weights, "seq", axis=1, tiled=True)
    projected = jnp.einsum("ltd,dc->ltc", width_deltas, weights, preferred_element_type=F32)
    per_column = jnp.sum(projected * grad_rows.astype(F32)[None], axis=1)
    partial_value = jnp.sum(per_column.reshape(layer_count, grad_rows.shape[1] // HD, HD), axis=2)
    totals = lax.psum(partial_value * norm, ("seq", "head"))
    placing = (layer_slot[:, None] == jnp.arange(layer_count, dtype=jnp.int32)[None, :]).astype(F32)
    scores = jnp.dot(placing.T, totals, precision=lax.Precision.HIGHEST)
    return grad_query, grad_keyval, scores


def solution(mesh):
    return jax.shard_map(
        on_device,
        mesh=mesh,
        in_specs=(
            P("seq", "head"),
            P("seq", "head"),
            P("seq", "head"),
            P("seq"),
            P("head", "seq", None),
            P("head", "seq"),
            P(),
        ),
        out_specs=(P("seq", "head"), P("seq", "head"), P()),
        check_vma=False,
    )
```

```python
import functools
import math

import jax
import jax.numpy as jnp
from jax import lax
from jax.experimental import pallas as pl
from jax.experimental.pallas import tpu as pltpu
from jax.sharding import PartitionSpec as P

H = 64
KVH = 8
HD = 128
DOC_ROWS = 16
NEG = -1e30
ANY = pl.BlockSpec(memory_space=pl.ANY)
SMEM = pl.BlockSpec(memory_space=pltpu.SMEM)
VMEM = pl.BlockSpec(memory_space=pltpu.VMEM)
F32 = jnp.float32
BF16 = jnp.bfloat16


def head_of(member, members, per_head):
    fold = min(per_head, members)
    return lax.div(member, fold) + lax.rem(member, fold) * (members // fold)


def cols(index, width):
    return pl.ds(pl.multiple_of(index * width, width), width)


def run_copies(copies):
    for copy in copies:
        copy.start()
    for copy in copies:
        copy.wait()


def by_halves(outs, members):
    half = max(members // 2, 1)
    return [outs[r // half].at[r % half] for r in range(members)]


def half_shapes(members, shape, dtype):
    half = max(members // 2, 1)
    return [jax.ShapeDtypeStruct((half,) + shape, dtype)] * (members // half)


def pack_keys_kernel(members, per_head, place_ref, doc_ref, kv_ref, *outs):
    tok = kv_ref.shape[0]
    ids = (doc_ref[...] + 1).astype(F32)
    ids = jnp.concatenate([ids] * (2 * HD // tok), axis=1)
    for r, out in enumerate(by_halves(outs, members)):
        head = head_of(place_ref[0] ^ r, members, per_head)
        out[:tok, :] = kv_ref[:, cols(head, 2 * HD)]
        out[tok:, :] = jnp.broadcast_to(ids, (DOC_ROWS, 2 * HD)).astype(BF16)


def pack_keys(place, doc_ids, keyval, members, per_head):
    tok = keyval.shape[0]
    shapes = half_shapes(members, (tok + DOC_ROWS, 2 * HD), BF16)
    return pl.pallas_call(
        functools.partial(pack_keys_kernel, members, per_head),
        out_shape=shapes,
        in_specs=[SMEM, VMEM, VMEM],
        out_specs=[VMEM] * len(shapes),
        name="pack_keys",
    )(place, doc_ids.reshape(1, tok), keyval)


def pack_queries_kernel(members, per_head, width, n_after, place_ref, q_ref, o_ref, *refs):
    outs = refs[n_after:]
    tok = q_ref.shape[0]
    for r, out in enumerate(by_halves(outs, members)):
        if r == 0 and members > 2:
            continue
        head = head_of(place_ref[0] ^ r, members, per_head)
        out[:tok, :] = q_ref[:, cols(head, width)]
        out[tok:, :] = o_ref[:, cols(head, width)]


def pack_queries(place, queries, grad_out, members, per_head, width, after):
    shapes = half_shapes(members, (2 * queries.shape[0], width), BF16)
    return pl.pallas_call(
        functools.partial(pack_queries_kernel, members, per_head, width, len(after)),
        out_shape=shapes,
        in_specs=[SMEM, VMEM, VMEM] + [ANY] * len(after),
        out_specs=[VMEM] * len(shapes),
        name="pack_queries",
    )(place, queries, grad_out, *after)


def join(views, after=()):
    arrays = [array for array, _ in views]

    def kernel(*refs):
        for k, (ref, (_, slot)) in enumerate(zip(refs, views)):
            refs[-1][k] = ref[slot]

    return pl.pallas_call(
        kernel,
        out_shape=jax.ShapeDtypeStruct((len(views),) + arrays[0].shape[1:], arrays[0].dtype),
        in_specs=[VMEM] * (len(views) + len(after)),
        out_specs=VMEM,
        name="join",
    )(*arrays, *after)


def split_kernel(place_ref, d_ref, mine_ref, theirs_ref):
    width = mine_ref.shape[1]
    mine_ref[...] = d_ref[:, cols(place_ref[1], width)]
    theirs_ref[...] = d_ref[:, cols(1 - place_ref[1], width)]


def split_width(place, rows):
    half = jax.ShapeDtypeStruct((rows.shape[0], rows.shape[1] // 2), BF16)
    return pl.pallas_call(
        split_kernel,
        out_shape=[half, half],
        in_specs=[SMEM, VMEM],
        out_specs=[VMEM, VMEM],
        name="split_deltas",
    )(place, rows)


def attention_kernel(members, per_head, group_size, tok, back, window, qo_slots, n_after, *refs):
    n_kv = back + 1
    n_in = 2 + members + n_kv
    refs = refs[:n_in] + refs[n_in + n_after :]
    place_ref, q_ref, o_ref = refs[:3]
    qo_refs = [ref.at[k] for ref, k in zip(refs[3 : 2 + members], qo_slots, strict=True)]
    kv_refs = refs[2 + members : 2 + members + n_kv]
    outs = refs[2 + members + n_kv :]
    n_dq = min(members, 2)
    dq_outs = by_halves(outs[:n_dq], members)
    own_out, prev_outs = outs[n_dq], outs[n_dq + 1 : n_dq + 1 + back]
    qs, dos, kvs, docs, k_t, bias, dqs, dk, dv, sems = outs[n_dq + 1 + back :]
    plane = members * tok
    me = place_ref[0]
    width = group_size * HD
    tile = bias.shape[2]
    span = bias.shape[1]
    n_tiles = plane // tile
    copies = []

    def add(src, dst):
        copies.append(pltpu.make_async_copy(src, dst, sems.at[len(copies)]))

    def rows(shard, size=None):
        size = tok if size is None else size
        return pl.ds(pl.multiple_of(shard * size, size), size)

    for r in range(members):
        shard = me ^ r
        for b in range(n_kv):
            at = (back - b) * members + shard
            add(kv_refs[b].at[r, pl.ds(0, tok), :], kvs.at[rows(at), :])
            add(kv_refs[b].at[r, pl.ds(tok, DOC_ROWS), :], docs.at[rows(at, DOC_ROWS), :])
    head = head_of(me, members, per_head)
    add(q_ref.at[:, cols(head, width)], qs.at[rows(me), :])
    add(o_ref.at[:, cols(head, width)], dos.at[rows(me), :])
    for r in range(1, members):
        add(qo_refs[r - 1].at[pl.ds(0, tok), :], qs.at[rows(me ^ r), :])
        add(qo_refs[r - 1].at[pl.ds(tok, tok), :], dos.at[rows(me ^ r), :])
    for copy in copies:
        copy.start()
    dk[...] = jnp.zeros_like(dk)
    dv[...] = jnp.zeros_like(dv)
    for copy in copies[: 2 * members * n_kv]:
        copy.wait()

    n_blocks = n_kv * plane // tok
    eye = lax.broadcasted_iota(jnp.int32, (tok, tok), 0) == lax.broadcasted_iota(jnp.int32, (tok, tok), 1)
    for b in range(n_blocks):
        k_t[:, b * tok : (b + 1) * tok] = kvs[b * tok : (b + 1) * tok, :HD].astype(F32).T.astype(BF16)
    first = back * plane - window

    def doc_row(b):
        return docs[b * DOC_ROWS : (b + 1) * DOC_ROWS, :tok].astype(F32)[:1]

    for b in range(n_blocks):
        column = jnp.sum(jnp.where(eye, jnp.broadcast_to(doc_row(b), (tok, tok)), 0.0), axis=1, keepdims=True)
        for i in range(n_tiles):
            low = first + i * tile
            if b * tok < low or b * tok >= low + span:
                continue
            at = b * tok - low
            here = back * plane + i * tile
            q_row = jnp.concatenate([doc_row(here // tok + k) for k in range(tile // tok)], axis=1)
            key_pos = b * tok + lax.broadcasted_iota(jnp.int32, (tok, tile), 0)
            query_pos = here + lax.broadcasted_iota(jnp.int32, (tok, tile), 1)
            ok = (column == q_row) & (key_pos <= query_pos)
            bias[i, at : at + tok, :] = jnp.where(ok, 0.0, NEG)
    for copy in copies[2 * members * n_kv :]:
        copy.wait()

    scale = 1.0 / math.sqrt(HD)
    to_log2 = scale * math.log2(math.e)
    nt = (((1,), (1,)), ((), ()))

    def one_head(h, _):
        at_h = cols(h, HD)
        for i in range(n_tiles):
            low = first + i * tile
            q = qs[i * tile : (i + 1) * tile, at_h]
            do = dos[i * tile : (i + 1) * tile, at_h]
            keys = kvs[low : low + span, :HD]
            values = kvs[low : low + span, HD:]
            st = lax.dot_general(keys, q, nt, preferred_element_type=F32) * to_log2 + bias[i]
            top = jnp.max(st, axis=0, keepdims=True)
            e = jnp.exp2(st - top)
            inv = 1.0 / jnp.sum(e, axis=0, keepdims=True)
            dpt = lax.dot_general(values, do, nt, preferred_element_type=F32)
            p = e * inv
            row_dot = jnp.sum(p * dpt, axis=0, keepdims=True)
            ds = (p * (dpt - row_dot)).astype(BF16)
            dv[low : low + span, :] += jnp.dot(p.astype(BF16), do, preferred_element_type=F32)
            dk[low : low + span, :] += jnp.dot(ds, q, preferred_element_type=F32)
            dqt = jnp.dot(k_t[:, low : low + span], ds, preferred_element_type=F32)
            dqs[i * tile : (i + 1) * tile, at_h] = (dqt.T * scale).astype(BF16)
        return 0

    lax.fori_loop(0, group_size, one_head, 0)
    own_out[:, :HD] = dk[back * plane :, :] * scale
    own_out[:, HD:] = dv[back * plane :, :]
    for b in range(1, n_kv):
        low = (back - b) * plane
        prev_outs[b - 1][:, :HD] = (dk[low : low + plane, :] * scale).astype(BF16)
        prev_outs[b - 1][:, HD:] = dv[low : low + plane, :].astype(BF16)
    run_copies(
        [pltpu.make_async_copy(dqs.at[rows(me ^ r), :], dq_outs[r], sems.at[r]) for r in range(members)]
    )


def attention(place, queries, grad_out, qo, kv, members, per_head, group_size, window, after):
    tok = queries.shape[0]
    plane = members * tok
    back = len(kv) - 1
    tile = min(256, plane)
    span = window + tile
    keys = (back + 1) * plane
    width = group_size * HD
    n_copies = 2 * members * len(kv) + 2 * members
    flops = 2 * group_size * plane * span * HD
    dq_shapes = half_shapes(members, (tok, width), BF16)
    return pl.pallas_call(
        functools.partial(
            attention_kernel, members, per_head, group_size, tok, back, window, [k for _, k in qo], len(after)
        ),
        out_shape=dq_shapes
        + [jax.ShapeDtypeStruct((plane, 2 * HD), F32)]
        + [jax.ShapeDtypeStruct((plane, 2 * HD), BF16)] * back,
        in_specs=[SMEM] + [ANY] * (2 + len(qo) + len(kv) + len(after)),
        out_specs=[ANY] * len(dq_shapes) + [VMEM] * (1 + back),
        scratch_shapes=[
            pltpu.VMEM((plane, width), BF16),
            pltpu.VMEM((plane, width), BF16),
            pltpu.VMEM((keys, 2 * HD), BF16),
            pltpu.VMEM((keys // tok * DOC_ROWS, 2 * HD), BF16),
            pltpu.VMEM((HD, keys), BF16),
            pltpu.VMEM((plane // tile, span, tile), F32),
            pltpu.VMEM((plane, width), BF16),
            pltpu.VMEM((keys, HD), F32),
            pltpu.VMEM((keys, HD), F32),
            pltpu.SemaphoreType.DMA((n_copies,)),
        ],
        compiler_params=pltpu.CompilerParams(vmem_limit_bytes=18 * 2**20),
        cost_estimate=pl.CostEstimate(
            flops=flops, bytes_accessed=6 * plane * width, transcendentals=group_size * plane * span
        ),
        name="attention_both_ways",
    )(place, queries, grad_out, *[array for array, _ in qo], *kv, *after)


def combine_kernel(members, tok, n_prev, place_ref, own_ref, *refs):
    prev, outs = refs[:n_prev], refs[n_prev:]
    token_outs, part_outs = by_halves(outs[:-3], members), outs[-3:-1]
    total = outs[-1]
    g = own_ref[...]
    for part in prev:
        g = g + part[...].astype(F32)
    total[...] = g.astype(BF16)
    me = place_ref[0]
    kind = lax.rem(me, 2)
    part_outs[0][...] = total[:, cols(kind, HD)]
    part_outs[1][...] = total[:, cols(1 - kind, HD)]
    for r in range(members):
        token_outs[r][...] = total[pl.ds(pl.multiple_of((me ^ r) * tok, tok), tok), :]


def combine(place, own, prev, members, tok, after):
    plane = own.shape[0]
    n_after = len(after)
    shapes = half_shapes(members, (tok, 2 * HD), BF16)

    def kernel(place_ref, own_ref, *refs):
        combine_kernel(members, tok, len(prev), place_ref, own_ref, *refs[: len(prev)], *refs[len(prev) + n_after :])

    return pl.pallas_call(
        kernel,
        out_shape=shapes + [jax.ShapeDtypeStruct((plane, HD), BF16)] * 2,
        in_specs=[SMEM] + [VMEM] * (1 + len(prev) + n_after),
        out_specs=[VMEM] * (len(shapes) + 2),
        scratch_shapes=[pltpu.VMEM((plane, 2 * HD), BF16)],
        name="sum_key_value_gradients",
    )(place, own, *prev, *after)


def settle_kernel(members, per_head, slots, place_ref, *refs):
    pieces = [ref.at[k] for ref, k in zip(refs[: 2 * members], slots, strict=True)]
    out_q, out_kv = refs[2 * members :]
    for r in range(members):
        head = head_of(place_ref[0] ^ r, members, per_head)
        for piece, out in ((pieces[r], out_q), (pieces[members + r], out_kv)):
            out[:, cols(head, piece.shape[1])] = piece[...]


def settle(place, dq, dkv, per_head):
    members = len(dq)
    tok = dq[0][0].shape[1]
    pieces = dq + dkv
    return pl.pallas_call(
        functools.partial(settle_kernel, members, per_head, [k for _, k in pieces]),
        out_shape=[
            jax.ShapeDtypeStruct((tok, members * part[0][0].shape[2]), BF16) for part in (dq, dkv)
        ],
        in_specs=[SMEM] + [VMEM] * (2 * members),
        out_specs=[VMEM, VMEM],
        name="place_heads",
    )(place, *[array for array, _ in pieces])


def project_kernel(layout, place_ref, *refs):
    d_refs, w_refs = refs[:4], list(refs[4:-2])
    out_ref, ws = refs[-2:]
    me, plane_at = place_ref[0], place_ref[2]
    layers, tok, depth = d_refs[0].shape
    for k, counts in enumerate(layout):
        end = 0
        for count in counts:
            start, end = end, end + min(w_ref.shape[0] for w_ref in w_refs[:count])
            rows, size = slice(start, end), end - start
            for z in range(count):
                w_ref = w_refs.pop(0)

                @pl.when(jnp.logical_or(count == 1, plane_at == z))
                def _():
                    ws[rows, k * HD : (k + 1) * HD] = w_ref[...] if w_ref.shape[0] == size else w_ref[rows, :]

    for r, d_ref in enumerate(d_refs):
        rows = d_ref[...].reshape(layers * tok, depth)
        out = jnp.dot(rows, ws[...], preferred_element_type=F32)
        for layer in range(layers):
            shard = layer * len(d_refs) + (me ^ r)
            out_ref[pl.ds(pl.multiple_of(shard * tok, tok), tok), :] = out[layer * tok : (layer + 1) * tok]


def project(place, pieces, blocks):
    layers, tok, depth = pieces[0].shape
    rows, width = layers * tok * len(pieces), HD * len(blocks)
    arrays = [array for block in blocks for part in block for array in part]
    return pl.pallas_call(
        functools.partial(project_kernel, [[len(part) for part in block] for block in blocks]),
        out_shape=jax.ShapeDtypeStruct((rows, width), F32),
        in_specs=[SMEM] + [VMEM] * (len(pieces) + len(arrays)),
        out_specs=VMEM,
        scratch_shapes=[pltpu.VMEM((depth, width), BF16)],
        compiler_params=pltpu.CompilerParams(vmem_limit_bytes=20 * 2**20),
        cost_estimate=pl.CostEstimate(
            flops=2 * rows * depth * width, bytes_accessed=2 * depth * (rows + width), transcendentals=0
        ),
        name="project_deltas",
    )(place, *pieces, *arrays)


def contract_kernel(norm, place_ref, slot_ref, p_ref, g0, g1, g2, g3, out_ref):
    me, side, plane_at = place_ref[0], place_ref[1], place_ref[2]
    kind = lax.rem(me, 2)
    shape = out_ref.shape[1:]
    row = lax.broadcasted_iota(jnp.int32, shape, 0)
    lane = lax.broadcasted_iota(jnp.int32, shape, 1)
    total = jnp.zeros(shape, F32)
    n_tok = g0.shape[0]
    for k, g_ref in enumerate((g0, g1, g2, g3)):
        block = 2 * (side ^ (k // 2)) + (kind ^ (k % 2))
        far = jnp.where(plane_at < 2, 2, 1)
        slot = jnp.where(
            block == plane_at, 0, jnp.where(block == (plane_at ^ 1), 1, jnp.where(block == far, 2, 3))
        )
        g = g_ref[...].astype(F32)
        for layer in range(2):
            rows = slice(layer * n_tok, (layer + 1) * n_tok)
            part = p_ref[rows, cols(slot, HD)] * g
            value = jnp.sum(jnp.sum(part, axis=0, keepdims=True), axis=1, keepdims=True) * norm
            here = (row == slot_ref[side ^ layer]) & (lane == 4 * block + me)
            total = total + jnp.where(here, value, 0.0)
    out_ref[...] = jnp.broadcast_to(total[None], out_ref.shape)


def contract(place, layer_slot, projected, parts, norm, n_dev):
    return pl.pallas_call(
        functools.partial(contract_kernel, norm),
        out_shape=jax.ShapeDtypeStruct((n_dev, 8, HD), F32),
        in_specs=[SMEM, SMEM] + [VMEM] * 5,
        out_specs=VMEM,
        compiler_params=pltpu.CompilerParams(vmem_limit_bytes=16 * 2**20),
        name="contract_scores",
    )(place, layer_slot, projected, *parts)


def on_device(queries, keyval, grad_out, doc_ids, deltas, node_weights, layer_slot):
    tok = queries.shape[0]
    members = keyval.shape[1] // (2 * HD)
    group_size = H // KVH
    n_seq, n_head = lax.axis_size("seq"), lax.axis_size("head")
    planes = n_seq // members
    plane_tok = members * tok
    window = n_seq * tok // 2
    back = -(-window // plane_tok)
    block_width = node_weights.shape[1]
    per_head = 2 * HD // block_width
    at_seq, at_head = lax.axis_index("seq"), lax.axis_index("head")
    place = jnp.stack([lax.rem(at_seq, members), at_head, lax.div(at_seq, members)]).astype(jnp.int32)

    def to_member(x, r):
        return lax.ppermute(x, "seq", [(s, s - s % members + ((s % members) ^ r)) for s in range(n_seq)])

    def to_plane(x, pairs):
        return lax.ppermute(
            x, "seq", [(a * members + k, b * members + k) for a, b in pairs for k in range(members)]
        )

    def shift(x, step):
        return to_plane(x, [(a, a + step) for a in range(planes) if 0 <= a + step < planes])

    def other_head(x):
        return lax.ppermute(x, "head", [(0, 1), (1, 0)])

    def other_head_and_member(x):
        pairs = [(2 * s + h, 2 * (s ^ 1) + (h ^ 1)) for s in range(n_seq) for h in range(2)]
        return lax.ppermute(x, ("seq", "head"), pairs)

    def follow(x, after):
        return lax.optimization_barrier((x, *after))[0] if after else x

    def exchange(halves, before=(), between=(), gate=None):
        if members == 1:
            return [(halves[0], 0)]
        bit = members // 2
        got = to_member(follow(halves[1], before), bit)
        views = [(halves[0], r) for r in range(bit)] + [(got, r) for r in range(bit)]
        while bit > 1:
            bit //= 2
            chosen = [r for r in range(members) if r & bit]
            chosen_views = [views[r] for r in chosen]
            message = join(chosen_views, gate) if gate else jnp.stack([array[k] for array, k in chosen_views])
            got = to_member(follow(message, between), bit)
            for k, r in enumerate(chosen):
                views[r] = (got, k)
        return views

    spread = n_head == 2 and members == 4 and planes == 4 and per_head == 2 and deltas.shape[0] == 1
    first, second, third = [], [], []
    if spread:
        pairs, middle, ends = [(0, 1), (1, 0), (2, 3), (3, 2)], [(1, 2), (2, 1)], [(1, 0), (2, 3)]
        w_pair, w_middle = to_plane(node_weights, pairs), to_plane(node_weights, middle)
        first = [w_pair, w_middle]
        mine, theirs = split_width(place, deltas.reshape(tok, deltas.shape[2]))
        crossed = other_head(theirs)

    keys = exchange(pack_keys(place, doc_ids, keyval, members, per_head))
    kv_plane = jnp.stack([array[k] for array, k in keys])
    ready = follow(kv_plane, first)
    kv = [kv_plane] + [shift(ready, k) for k in range(1, back + 1)]
    queries_out = pack_queries(place, queries, grad_out, members, per_head, group_size * HD, ())
    qo = exchange(queries_out, [array for array, _ in keys[1:]], kv[1:])

    if spread:
        near = jnp.stack([mine, crossed])
        other = to_member(follow(near, [qo[-2][0]] + kv[1:]), 2)
        near_c = to_member(near, 1)
        w_ends = to_plane(follow(w_middle, kv[1:]), ends)
        w_middle2 = to_plane(follow(w_pair, kv[1:]), middle)
        w_ends2 = to_plane(follow(w_pair, kv[1:]), [(1, 3), (2, 0)])
        second = [w_ends, w_middle2, w_ends2]

    out = attention(place, queries, grad_out, qo[1:], kv, members, per_head, group_size, window, ())
    n_dq = min(members, 2)
    dq, own, prev = out[:n_dq], out[n_dq], out[n_dq + 1 :]
    prev = [shift(follow(prev[k], second), -(k + 1)) for k in range(back)]
    if spread:
        other_c = to_member(follow(other, second + [own]), 1)
        pieces = [near, near_c, other, other_c]
    if spread:
        sides = (w_ends, w_middle, w_middle, w_ends)
        last = (w_ends2, w_middle2, w_middle2, w_ends2)
        projected = project(place, pieces, [[(node_weights,)], [(w_pair,)], [sides], [last]])
        third = [projected]
    summed = combine(place, own, prev, members, tok, third)
    token_parts, kinds = summed[:-2], summed[-2:]
    norm = 1.0 / math.sqrt(n_seq * tok)
    partial = []
    if spread:
        parts = [kinds[0], to_member(kinds[1], 1), other_head(kinds[0]), other_head_and_member(kinds[1])]
        partial = [contract(place, layer_slot, projected, parts, norm, n_seq * n_head)]
    dq = exchange(dq, gate=partial)
    dkv = exchange(token_parts, gate=partial)
    grad_query, grad_keyval = settle(place, dq, dkv, per_head)
    if spread:
        copies = lax.all_to_all(partial[0], ("seq", "head"), 0, 0, tiled=True)
        scores = jnp.sum(copies, axis=0)[: layer_slot.shape[0], : n_seq * block_width // HD]
        return grad_query, grad_keyval, scores

    width_deltas = lax.all_to_all(deltas, "head", split_axis=2, concat_axis=0, tiled=True)
    grad_rows = lax.all_gather(grad_keyval, "head", axis=1, tiled=True)
    layer_count = width_deltas.shape[0]
    weights = lax.all_gather(node_weights, "seq", axis=1, tiled=True)
    projected = jnp.einsum("ltd,dc->ltc", width_deltas, weights, preferred_element_type=F32)
    per_column = jnp.sum(projected * grad_rows.astype(F32)[None], axis=1)
    partial_value = jnp.sum(per_column.reshape(layer_count, grad_rows.shape[1] // HD, HD), axis=2)
    totals = lax.psum(partial_value * norm, ("seq", "head"))
    placing = (layer_slot[:, None] == jnp.arange(layer_count, dtype=jnp.int32)[None, :]).astype(F32)
    scores = jnp.dot(placing.T, totals, precision=lax.Precision.HIGHEST)
    return grad_query, grad_keyval, scores


def solution(mesh):
    return jax.shard_map(
        on_device,
        mesh=mesh,
        in_specs=(
            P("seq", "head"),
            P("seq", "head"),
            P("seq", "head"),
            P("seq"),
            P("head", "seq", None),
            P("head", "seq"),
            P(),
        ),
        out_specs=(P("seq", "head"), P("seq", "head"), P()),
        check_vma=False,
    )
```

```python
import functools
import math

import jax
import jax.numpy as jnp
from jax import lax
from jax.experimental import pallas as pl
from jax.experimental.pallas import tpu as pltpu
from jax.sharding import PartitionSpec as P

H = 64
KVH = 8
HD = 128
DOC_ROWS = 16
NEG = -1e30
ANY = pl.BlockSpec(memory_space=pl.ANY)
SMEM = pl.BlockSpec(memory_space=pltpu.SMEM)
VMEM = pl.BlockSpec(memory_space=pltpu.VMEM)
F32 = jnp.float32
BF16 = jnp.bfloat16


def head_of(member, members, per_head):
    fold = min(per_head, members)
    return lax.div(member, fold) + lax.rem(member, fold) * (members // fold)


def cols(index, width):
    return pl.ds(pl.multiple_of(index * width, width), width)


def run_copies(copies):
    for copy in copies:
        copy.start()
    for copy in copies:
        copy.wait()


def by_halves(outs, members):
    half = max(members // 2, 1)
    return [outs[r // half].at[r % half] for r in range(members)]


def half_shapes(members, shape, dtype):
    half = max(members // 2, 1)
    return [jax.ShapeDtypeStruct((half,) + shape, dtype)] * (members // half)


def pack_keys_kernel(members, per_head, place_ref, doc_ref, kv_ref, *outs):
    tok = kv_ref.shape[0]
    ids = (doc_ref[...] + 1).astype(F32)
    ids = jnp.concatenate([ids] * (2 * HD // tok), axis=1)
    for r, out in enumerate(by_halves(outs, members)):
        head = head_of(place_ref[0] ^ r, members, per_head)
        out[:tok, :] = kv_ref[:, cols(head, 2 * HD)]
        out[tok:, :] = jnp.broadcast_to(ids, (DOC_ROWS, 2 * HD)).astype(BF16)


def pack_keys(place, doc_ids, keyval, members, per_head):
    tok = keyval.shape[0]
    shapes = half_shapes(members, (tok + DOC_ROWS, 2 * HD), BF16)
    return pl.pallas_call(
        functools.partial(pack_keys_kernel, members, per_head),
        out_shape=shapes,
        in_specs=[SMEM, VMEM, VMEM],
        out_specs=[VMEM] * len(shapes),
        name="pack_keys",
    )(place, doc_ids.reshape(1, tok), keyval)


def pack_queries_kernel(members, per_head, width, n_after, place_ref, q_ref, o_ref, *refs):
    outs = refs[n_after:]
    tok = q_ref.shape[0]
    for r, out in enumerate(by_halves(outs, members)):
        if r == 0 and members > 2:
            continue
        head = head_of(place_ref[0] ^ r, members, per_head)
        out[:tok, :] = q_ref[:, cols(head, width)]
        out[tok:, :] = o_ref[:, cols(head, width)]


def pack_queries(place, queries, grad_out, members, per_head, width, after):
    shapes = half_shapes(members, (2 * queries.shape[0], width), BF16)
    return pl.pallas_call(
        functools.partial(pack_queries_kernel, members, per_head, width, len(after)),
        out_shape=shapes,
        in_specs=[SMEM, VMEM, VMEM] + [ANY] * len(after),
        out_specs=[VMEM] * len(shapes),
        name="pack_queries",
    )(place, queries, grad_out, *after)


def join(views, after=()):
    arrays = [array for array, _ in views]

    def kernel(*refs):
        for k, (ref, (_, slot)) in enumerate(zip(refs, views)):
            refs[-1][k] = ref[slot]

    return pl.pallas_call(
        kernel,
        out_shape=jax.ShapeDtypeStruct((len(views),) + arrays[0].shape[1:], arrays[0].dtype),
        in_specs=[VMEM] * (len(views) + len(after)),
        out_specs=VMEM,
        name="join",
    )(*arrays, *after)


def split_kernel(place_ref, d_ref, mine_ref, theirs_ref):
    width = mine_ref.shape[1]
    mine_ref[...] = d_ref[:, cols(place_ref[1], width)]
    theirs_ref[...] = d_ref[:, cols(1 - place_ref[1], width)]


def split_width(place, rows):
    half = jax.ShapeDtypeStruct((rows.shape[0], rows.shape[1] // 2), BF16)
    return pl.pallas_call(
        split_kernel,
        out_shape=[half, half],
        in_specs=[SMEM, VMEM],
        out_specs=[VMEM, VMEM],
        name="split_deltas",
    )(place, rows)


def attention_kernel(members, per_head, group_size, tok, back, window, qo_slots, n_after, *refs):
    n_kv = back + 1
    n_in = 2 + members + n_kv
    refs = refs[:n_in] + refs[n_in + n_after :]
    place_ref, q_ref, o_ref = refs[:3]
    qo_refs = [ref.at[k] for ref, k in zip(refs[3 : 2 + members], qo_slots, strict=True)]
    kv_refs = refs[2 + members : 2 + members + n_kv]
    outs = refs[2 + members + n_kv :]
    n_dq = min(members, 2)
    dq_outs = by_halves(outs[:n_dq], members)
    own_out, prev_outs = outs[n_dq], outs[n_dq + 1 : n_dq + 1 + back]
    qs, dos, kvs, docs, k_t, bias, dqs, dk, dv, sems = outs[n_dq + 1 + back :]
    plane = members * tok
    me = place_ref[0]
    width = group_size * HD
    tile = bias.shape[2]
    span = bias.shape[1]
    n_tiles = plane // tile
    copies = []

    def add(src, dst):
        copies.append(pltpu.make_async_copy(src, dst, sems.at[len(copies)]))

    def rows(shard, size=None):
        size = tok if size is None else size
        return pl.ds(pl.multiple_of(shard * size, size), size)

    for r in range(members):
        shard = me ^ r
        for b in range(n_kv):
            at = (back - b) * members + shard
            add(kv_refs[b].at[r, pl.ds(0, tok), :], kvs.at[rows(at), :])
            add(kv_refs[b].at[r, pl.ds(tok, DOC_ROWS), :], docs.at[rows(at, DOC_ROWS), :])
    head = head_of(me, members, per_head)
    add(q_ref.at[:, cols(head, width)], qs.at[rows(me), :])
    add(o_ref.at[:, cols(head, width)], dos.at[rows(me), :])
    for r in range(1, members):
        add(qo_refs[r - 1].at[pl.ds(0, tok), :], qs.at[rows(me ^ r), :])
        add(qo_refs[r - 1].at[pl.ds(tok, tok), :], dos.at[rows(me ^ r), :])
    for copy in copies:
        copy.start()
    dk[...] = jnp.zeros_like(dk)
    dv[...] = jnp.zeros_like(dv)
    for copy in copies[: 2 * members * n_kv]:
        copy.wait()

    n_blocks = n_kv * plane // tok
    eye = lax.broadcasted_iota(jnp.int32, (tok, tok), 0) == lax.broadcasted_iota(jnp.int32, (tok, tok), 1)
    for b in range(n_blocks):
        k_t[:, b * tok : (b + 1) * tok] = kvs[b * tok : (b + 1) * tok, :HD].astype(F32).T.astype(BF16)
    first = back * plane - window

    def doc_row(b):
        return docs[b * DOC_ROWS : (b + 1) * DOC_ROWS, :tok].astype(F32)[:1]

    for b in range(n_blocks):
        column = jnp.sum(jnp.where(eye, jnp.broadcast_to(doc_row(b), (tok, tok)), 0.0), axis=1, keepdims=True)
        for i in range(n_tiles):
            low = first + i * tile
            if b * tok < low or b * tok >= low + span:
                continue
            at = b * tok - low
            here = back * plane + i * tile
            q_row = jnp.concatenate([doc_row(here // tok + k) for k in range(tile // tok)], axis=1)
            key_pos = b * tok + lax.broadcasted_iota(jnp.int32, (tok, tile), 0)
            query_pos = here + lax.broadcasted_iota(jnp.int32, (tok, tile), 1)
            ok = (column == q_row) & (key_pos <= query_pos)
            bias[i, at : at + tok, :] = jnp.where(ok, 0.0, NEG)
    for copy in copies[2 * members * n_kv :]:
        copy.wait()

    scale = 1.0 / math.sqrt(HD)
    to_log2 = scale * math.log2(math.e)
    nt = (((1,), (1,)), ((), ()))

    def one_head(h, _):
        at_h = cols(h, HD)
        for i in range(n_tiles):
            low = first + i * tile
            q = qs[i * tile : (i + 1) * tile, at_h]
            do = dos[i * tile : (i + 1) * tile, at_h]
            keys = kvs[low : low + span, :HD]
            values = kvs[low : low + span, HD:]
            st = lax.dot_general(keys, q, nt, preferred_element_type=F32) * to_log2 + bias[i]
            top = jnp.max(st, axis=0, keepdims=True)
            e = jnp.exp2(st - top)
            inv = 1.0 / jnp.sum(e, axis=0, keepdims=True)
            dpt = lax.dot_general(values, do, nt, preferred_element_type=F32)
            p = e * inv
            row_dot = jnp.sum(p * dpt, axis=0, keepdims=True)
            ds = (p * (dpt - row_dot)).astype(BF16)
            dv[low : low + span, :] += jnp.dot(p.astype(BF16), do, preferred_element_type=F32)
            dk[low : low + span, :] += jnp.dot(ds, q, preferred_element_type=F32)
            dqt = jnp.dot(k_t[:, low : low + span], ds, preferred_element_type=F32)
            dqs[i * tile : (i + 1) * tile, at_h] = (dqt.T * scale).astype(BF16)
        return 0

    lax.fori_loop(0, group_size, one_head, 0)
    own_out[:, :HD] = dk[back * plane :, :] * scale
    own_out[:, HD:] = dv[back * plane :, :]
    for b in range(1, n_kv):
        low = (back - b) * plane
        prev_outs[b - 1][:, :HD] = (dk[low : low + plane, :] * scale).astype(BF16)
        prev_outs[b - 1][:, HD:] = dv[low : low + plane, :].astype(BF16)
    run_copies(
        [pltpu.make_async_copy(dqs.at[rows(me ^ r), :], dq_outs[r], sems.at[r]) for r in range(members)]
    )


def attention(place, queries, grad_out, qo, kv, members, per_head, group_size, window, after):
    tok = queries.shape[0]
    plane = members * tok
    back = len(kv) - 1
    tile = min(256, plane)
    span = window + tile
    keys = (back + 1) * plane
    width = group_size * HD
    n_copies = 2 * members * len(kv) + 2 * members
    flops = 2 * group_size * plane * span * HD
    dq_shapes = half_shapes(members, (tok, width), BF16)
    return pl.pallas_call(
        functools.partial(
            attention_kernel, members, per_head, group_size, tok, back, window, [k for _, k in qo], len(after)
        ),
        out_shape=dq_shapes
        + [jax.ShapeDtypeStruct((plane, 2 * HD), F32)]
        + [jax.ShapeDtypeStruct((plane, 2 * HD), BF16)] * back,
        in_specs=[SMEM] + [ANY] * (2 + len(qo) + len(kv) + len(after)),
        out_specs=[ANY] * len(dq_shapes) + [VMEM] * (1 + back),
        scratch_shapes=[
            pltpu.VMEM((plane, width), BF16),
            pltpu.VMEM((plane, width), BF16),
            pltpu.VMEM((keys, 2 * HD), BF16),
            pltpu.VMEM((keys // tok * DOC_ROWS, 2 * HD), BF16),
            pltpu.VMEM((HD, keys), BF16),
            pltpu.VMEM((plane // tile, span, tile), F32),
            pltpu.VMEM((plane, width), BF16),
            pltpu.VMEM((keys, HD), F32),
            pltpu.VMEM((keys, HD), F32),
            pltpu.SemaphoreType.DMA((n_copies,)),
        ],
        compiler_params=pltpu.CompilerParams(vmem_limit_bytes=18 * 2**20),
        cost_estimate=pl.CostEstimate(
            flops=flops, bytes_accessed=6 * plane * width, transcendentals=group_size * plane * span
        ),
        name="attention_both_ways",
    )(place, queries, grad_out, *[array for array, _ in qo], *kv, *after)


def combine_kernel(members, tok, n_prev, place_ref, own_ref, *refs):
    prev, outs = refs[:n_prev], refs[n_prev:]
    token_outs, part_outs = by_halves(outs[:-3], members), outs[-3:-1]
    total = outs[-1]
    g = own_ref[...]
    for part in prev:
        g = g + part[...].astype(F32)
    total[...] = g.astype(BF16)
    me = place_ref[0]
    kind = lax.rem(me, 2)
    part_outs[0][...] = total[:, cols(kind, HD)]
    part_outs[1][...] = total[:, cols(1 - kind, HD)]
    for r in range(members):
        token_outs[r][...] = total[pl.ds(pl.multiple_of((me ^ r) * tok, tok), tok), :]


def combine(place, own, prev, members, tok, after):
    plane = own.shape[0]
    n_after = len(after)
    shapes = half_shapes(members, (tok, 2 * HD), BF16)

    def kernel(place_ref, own_ref, *refs):
        combine_kernel(members, tok, len(prev), place_ref, own_ref, *refs[: len(prev)], *refs[len(prev) + n_after :])

    return pl.pallas_call(
        kernel,
        out_shape=shapes + [jax.ShapeDtypeStruct((plane, HD), BF16)] * 2,
        in_specs=[SMEM] + [VMEM] * (1 + len(prev) + n_after),
        out_specs=[VMEM] * (len(shapes) + 2),
        scratch_shapes=[pltpu.VMEM((plane, 2 * HD), BF16)],
        name="sum_key_value_gradients",
    )(place, own, *prev, *after)


def settle_kernel(members, per_head, slots, place_ref, *refs):
    pieces = [ref.at[k] for ref, k in zip(refs[: 2 * members], slots, strict=True)]
    out_q, out_kv = refs[2 * members :]
    for r in range(members):
        head = head_of(place_ref[0] ^ r, members, per_head)
        for piece, out in ((pieces[r], out_q), (pieces[members + r], out_kv)):
            out[:, cols(head, piece.shape[1])] = piece[...]


def settle(place, dq, dkv, per_head):
    members = len(dq)
    tok = dq[0][0].shape[1]
    pieces = dq + dkv
    return pl.pallas_call(
        functools.partial(settle_kernel, members, per_head, [k for _, k in pieces]),
        out_shape=[
            jax.ShapeDtypeStruct((tok, members * part[0][0].shape[2]), BF16) for part in (dq, dkv)
        ],
        in_specs=[SMEM] + [VMEM] * (2 * members),
        out_specs=[VMEM, VMEM],
        name="place_heads",
    )(place, *[array for array, _ in pieces])


def project_kernel(layout, place_ref, *refs):
    d_refs, w_refs = refs[:4], list(refs[4:-2])
    out_ref, ws = refs[-2:]
    me, plane_at = place_ref[0], place_ref[2]
    layers, tok, depth = d_refs[0].shape
    for k, counts in enumerate(layout):
        end = 0
        for count in counts:
            start, end = end, end + min(w_ref.shape[0] for w_ref in w_refs[:count])
            rows, size = slice(start, end), end - start
            for z in range(count):
                w_ref = w_refs.pop(0)

                @pl.when(jnp.logical_or(count == 1, plane_at == z))
                def _():
                    ws[rows, k * HD : (k + 1) * HD] = w_ref[...] if w_ref.shape[0] == size else w_ref[rows, :]

    for r, d_ref in enumerate(d_refs):
        rows = d_ref[...].reshape(layers * tok, depth)
        out = jnp.dot(rows, ws[...], preferred_element_type=F32)
        for layer in range(layers):
            shard = layer * len(d_refs) + (me ^ r)
            out_ref[pl.ds(pl.multiple_of(shard * tok, tok), tok), :] = out[layer * tok : (layer + 1) * tok]


def project(place, pieces, blocks):
    layers, tok, depth = pieces[0].shape
    rows, width = layers * tok * len(pieces), HD * len(blocks)
    arrays = [array for block in blocks for part in block for array in part]
    return pl.pallas_call(
        functools.partial(project_kernel, [[len(part) for part in block] for block in blocks]),
        out_shape=jax.ShapeDtypeStruct((rows, width), F32),
        in_specs=[SMEM] + [VMEM] * (len(pieces) + len(arrays)),
        out_specs=VMEM,
        scratch_shapes=[pltpu.VMEM((depth, width), BF16)],
        compiler_params=pltpu.CompilerParams(vmem_limit_bytes=20 * 2**20),
        cost_estimate=pl.CostEstimate(
            flops=2 * rows * depth * width, bytes_accessed=2 * depth * (rows + width), transcendentals=0
        ),
        name="project_deltas",
    )(place, *pieces, *arrays)


def contract_kernel(norm, place_ref, slot_ref, p_ref, g0, g1, g2, g3, *refs):
    out_ref = refs[-1]
    me, side, plane_at = place_ref[0], place_ref[1], place_ref[2]
    kind = lax.rem(me, 2)
    shape = out_ref.shape[1:]
    row = lax.broadcasted_iota(jnp.int32, shape, 0)
    lane = lax.broadcasted_iota(jnp.int32, shape, 1)
    total = jnp.zeros(shape, F32)
    n_tok = g0.shape[0]
    for k, g_ref in enumerate((g0, g1, g2, g3)):
        block = 2 * (side ^ (k // 2)) + (kind ^ (k % 2))
        far = jnp.where(plane_at < 2, 2, 1)
        slot = jnp.where(
            block == plane_at, 0, jnp.where(block == (plane_at ^ 1), 1, jnp.where(block == far, 2, 3))
        )
        g = g_ref[...].astype(F32)
        for layer in range(2):
            rows = slice(layer * n_tok, (layer + 1) * n_tok)
            part = p_ref[rows, cols(slot, HD)] * g
            value = jnp.sum(jnp.sum(part, axis=0, keepdims=True), axis=1, keepdims=True) * norm
            here = (row == slot_ref[side ^ layer]) & (lane == 4 * block + me)
            total = total + jnp.where(here, value, 0.0)
    out_ref[...] = jnp.broadcast_to(total[None], out_ref.shape)


def contract(place, layer_slot, projected, parts, norm, n_dev, after):
    return pl.pallas_call(
        functools.partial(contract_kernel, norm),
        out_shape=jax.ShapeDtypeStruct((n_dev, 8, HD), F32),
        in_specs=[SMEM, SMEM] + [VMEM] * (5 + len(after)),
        out_specs=VMEM,
        compiler_params=pltpu.CompilerParams(vmem_limit_bytes=16 * 2**20),
        name="contract_scores",
    )(place, layer_slot, projected, *parts, *after)


def on_device(queries, keyval, grad_out, doc_ids, deltas, node_weights, layer_slot):
    tok = queries.shape[0]
    members = keyval.shape[1] // (2 * HD)
    group_size = H // KVH
    n_seq, n_head = lax.axis_size("seq"), lax.axis_size("head")
    planes = n_seq // members
    plane_tok = members * tok
    window = n_seq * tok // 2
    back = -(-window // plane_tok)
    block_width = node_weights.shape[1]
    per_head = 2 * HD // block_width
    at_seq, at_head = lax.axis_index("seq"), lax.axis_index("head")
    place = jnp.stack([lax.rem(at_seq, members), at_head, lax.div(at_seq, members)]).astype(jnp.int32)

    def to_member(x, r):
        return lax.ppermute(x, "seq", [(s, s - s % members + ((s % members) ^ r)) for s in range(n_seq)])

    def to_plane(x, pairs):
        return lax.ppermute(
            x, "seq", [(a * members + k, b * members + k) for a, b in pairs for k in range(members)]
        )

    def shift(x, step):
        return to_plane(x, [(a, a + step) for a in range(planes) if 0 <= a + step < planes])

    def other_head(x):
        return lax.ppermute(x, "head", [(0, 1), (1, 0)])

    def other_head_and_member(x):
        pairs = [(2 * s + h, 2 * (s ^ 1) + (h ^ 1)) for s in range(n_seq) for h in range(2)]
        return lax.ppermute(x, ("seq", "head"), pairs)

    def follow(x, after):
        return lax.optimization_barrier((x, *after))[0] if after else x

    def exchange(halves, before=(), between=(), gate=None):
        if members == 1:
            return [(halves[0], 0)]
        bit = members // 2
        got = to_member(follow(halves[1], before), bit)
        views = [(halves[0], r) for r in range(bit)] + [(got, r) for r in range(bit)]
        while bit > 1:
            bit //= 2
            chosen = [r for r in range(members) if r & bit]
            chosen_views = [views[r] for r in chosen]
            message = join(chosen_views, gate) if gate else jnp.stack([array[k] for array, k in chosen_views])
            got = to_member(follow(message, between), bit)
            for k, r in enumerate(chosen):
                views[r] = (got, k)
        return views

    spread = n_head == 2 and members == 4 and planes == 4 and per_head == 2 and deltas.shape[0] == 1
    first, second, third, down = [], [], [], []
    if spread:
        pairs, middle, ends = [(0, 1), (1, 0), (2, 3), (3, 2)], [(1, 2), (2, 1)], [(1, 0), (2, 3)]
        w_pair, w_middle = to_plane(node_weights, pairs), to_plane(node_weights, middle)
        first = [w_pair, w_middle]
        down = [to_plane(w_middle, [(1, 0)]), to_plane(w_pair, [(2, 1)])]
        mine, theirs = split_width(place, deltas.reshape(tok, deltas.shape[2]))
        crossed = other_head(theirs)

    keys = exchange(pack_keys(place, doc_ids, keyval, members, per_head))
    kv_plane = jnp.stack([array[k] for array, k in keys])
    ready = follow(kv_plane, first)
    kv = [kv_plane] + [shift(ready, k) for k in range(1, back + 1)]
    queries_out = pack_queries(place, queries, grad_out, members, per_head, group_size * HD, ())
    qo = exchange(queries_out, [array for array, _ in keys[1:]], kv[1:])

    if spread:
        near = jnp.stack([mine, crossed])
        other = to_member(follow(near, [qo[-2][0]] + kv[1:]), 2)
        near_c = to_member(near, 1)
        up = [to_plane(follow(w_middle, kv[1:]), [(2, 3)]), to_plane(follow(w_pair, kv[1:]), [(1, 2)])]
        up.append(to_plane(follow(w_pair, kv[1:]), [(1, 3)]))
        down.append(to_plane(follow(w_pair, kv[1:] + down), [(2, 0)]))
        second = up + down

    out = attention(place, queries, grad_out, qo[1:], kv, members, per_head, group_size, window, ())
    n_dq = min(members, 2)
    dq, own, prev = out[:n_dq], out[n_dq], out[n_dq + 1 :]
    prev = [shift(follow(prev[k], down), -(k + 1)) for k in range(back)]
    if spread:
        other_c = to_member(follow(other, second + [own]), 1)
        pieces = [near, near_c, other, other_c]
    if spread:
        sides = (down[0], w_middle, w_middle, up[0])
        last = (down[2], down[1], up[1], up[2])
        projected = project(place, pieces, [[(node_weights,)], [(w_pair,)], [sides], [last]])
        third = [projected]
    summed = combine(place, own, prev, members, tok, third)
    token_parts, kinds = summed[:-2], summed[-2:]
    norm = 1.0 / math.sqrt(n_seq * tok)
    if spread:
        parts = [kinds[0], to_member(kinds[1], 1), other_head(kinds[0]), other_head_and_member(kinds[1])]
    dq = exchange(dq, gate=[projected] if spread else ())
    dkv = exchange(token_parts)
    if spread:
        partial = contract(place, layer_slot, projected, parts, norm, n_seq * n_head, [dq[1][0], dkv[1][0]])
    grad_query, grad_keyval = settle(place, dq, dkv, per_head)
    if spread:
        copies = lax.all_to_all(partial, ("seq", "head"), 0, 0, tiled=True)
        scores = jnp.sum(copies, axis=0)[: layer_slot.shape[0], : n_seq * block_width // HD]
        return grad_query, grad_keyval, scores

    width_deltas = lax.all_to_all(deltas, "head", split_axis=2, concat_axis=0, tiled=True)
    grad_rows = lax.all_gather(grad_keyval, "head", axis=1, tiled=True)
    layer_count = width_deltas.shape[0]
    weights = lax.all_gather(node_weights, "seq", axis=1, tiled=True)
    projected = jnp.einsum("ltd,dc->ltc", width_deltas, weights, preferred_element_type=F32)
    per_column = jnp.sum(projected * grad_rows.astype(F32)[None], axis=1)
    partial_value = jnp.sum(per_column.reshape(layer_count, grad_rows.shape[1] // HD, HD), axis=2)
    totals = lax.psum(partial_value * norm, ("seq", "head"))
    placing = (layer_slot[:, None] == jnp.arange(layer_count, dtype=jnp.int32)[None, :]).astype(F32)
    scores = jnp.dot(placing.T, totals, precision=lax.Precision.HIGHEST)
    return grad_query, grad_keyval, scores


def solution(mesh):
    return jax.shard_map(
        on_device,
        mesh=mesh,
        in_specs=(
            P("seq", "head"),
            P("seq", "head"),
            P("seq", "head"),
            P("seq"),
            P("head", "seq", None),
            P("head", "seq"),
            P(),
        ),
        out_specs=(P("seq", "head"), P("seq", "head"), P()),
        check_vma=False,
    )
```
